512 devices in a mesh: slab: 32 (over z, core), chan: 16 (over x, y).
Axes of the slice: x: 4, y: 4, z: 16, core: 2. Of those that a mesh axis runs over, the one named last changes fastest.
Arguments:
- image_center: bfloat16 [256, 256, 2048], P('slab', None, 'chan'), may hold values from -6 to 6
- image_radius: bfloat16 [256, 256, 2048], P('slab', None, 'chan'), may hold values from 4.976988e-06 to 4.9829483e-05
- first_kernel: bfloat16 [3, 3, 256, 256], replicated, may hold values from -0.125 to 0.125
- first_bias: float32 [256], replicated, may hold values from -3 to 3
- second_kernel: bfloat16 [3, 3, 256, 256], replicated, may hold values from -0.125 to 0.125
- second_bias: float32 [256], replicated, may hold values from -3 to 3
- third_weight: bfloat16 [256, 256], replicated, may hold values from -0.375 to 0.375
- third_bias: float32 [256], replicated, may hold values from -3 to 3
- fourth_weight: bfloat16 [256, 256], replicated, may hold values from -0.375 to 0.375
- fourth_bias: float32 [256], replicated, may hold values from -3 to 3
- score_weight: bfloat16 [256], replicated, may hold values from -0.375 to 0.375
- score_bias: float32 [1], replicated, may hold values from -3 to 3
- tile_count: int32 [32, 16], P('slab', 'chan'), may hold values from 0 to 2, as said below
- tile_row: int32 [32, 16, 2], P('slab', 'chan'), may hold values from 0 to 7, as said below
- owner_slot: int32 [32, 16, 2], P('slab', 'chan'), may hold values from -1 to 255, as said below
Outputs:
- ibp_bounds: float32 [2, 256, 2048], P(None, 'slab', 'chan')
- refined: float32 [256, 2, 128], P('slab')
The draws below stay inside these ranges and needn't reach their ends.
Inputs may be any that keep to these rules, and one draw needn't show every extreme that they name: `tile_count`: each device holds 0 to 2 tiles in its first slots; in every draw some slab has 2 tiles on each of its devices, and the window holds exactly 256 tiles. `tile_row`: rows of the slots of one device are distinct; slots at or beyond the count are not used. `owner_slot`: slots below the count hold distinct global slots that cover all of 0 to 255; global slot g is kept by slab index g // 8; at most 1 tiles of one slab go to one slab index, and that many in every draw; slots at or beyond the count hold -1.
All inputs are finite; a program needn't handle non-finite values.
Results may differ from the reference program's by a relative error of at most 0.002.
The reference program's roundings to bfloat16 on the way (of `coeff_four` and `coeff_three`) count: a program that leaves them out, or rounds other values in their place, can miss the bound.
Values may be sent and summed in bfloat16 or wider, within the bound.
A program may use at most 64 MiB of HBM per device.

```python
import math
import jax
import jax.numpy as jnp
from jax import lax

C = 256
PIX = 128
ROWS_DEV = 8
TILES_DEV = 2
SLOT_CAP = 8
IMG_H = 256
IMG_W = 2048
N_SLAB = 32
N_CHAN = 16


def tile_plan(key):
    base = jax.random.fold_in(key, 7)
    keys = jax.random.split(base, 7)
    slot_total = N_SLAB * N_CHAN * TILES_DEV
    tiles_total = N_SLAB * SLOT_CAP
    heavy = jax.random.randint(keys[0], (), 0, N_SLAB)
    indices = jnp.arange(slot_total, dtype=jnp.int32)
    slab_of = indices // (N_CHAN * TILES_DEV)
    weights = jax.random.randint(keys[1], (N_SLAB,), 1, 9)
    noise = jax.random.randint(keys[2], (slot_total,), 0, 1024)
    scores = noise * weights[slab_of] * slot_total + indices
    scores = jnp.where(slab_of == heavy, 2 ** 30 + indices, scores)
    _, chosen = lax.top_k(scores, tiles_total)
    chosen_mask = jnp.zeros((slot_total,), jnp.int32).at[chosen].set(1)
    counts = chosen_mask.reshape(N_SLAB, N_CHAN, TILES_DEV).sum(axis=-1).astype(jnp.int32)
    row_keys = jax.random.randint(keys[3], (N_SLAB, N_CHAN, ROWS_DEV), 0, 2 ** 20) * ROWS_DEV
    row_keys = row_keys + jnp.arange(ROWS_DEV, dtype=jnp.int32)
    rows = jnp.argsort(row_keys, axis=-1)[..., :TILES_DEV].astype(jnp.int32)
    present = jnp.arange(TILES_DEV, dtype=jnp.int32)[None, None, :] < counts[:, :, None]
    present_flat = present.reshape(-1).astype(jnp.int32)
    ranks = jnp.cumsum(present_flat) - 1
    rotate = jax.random.randint(keys[4], (), 0, tiles_total)
    dealt = (ranks + rotate) % tiles_total
    owner_perm = jax.random.permutation(keys[5], N_SLAB).astype(jnp.int32)
    place_perm = jax.random.permutation(keys[6], SLOT_CAP).astype(jnp.int32)
    global_slot = owner_perm[dealt % N_SLAB] * SLOT_CAP + place_perm[dealt // N_SLAB]
    owners = jnp.where(present_flat > 0, global_slot, -1).reshape(N_SLAB, N_CHAN, TILES_DEV).astype(jnp.int32)
    return (counts, rows, owners)


def draw_tile_count(key, part):
    return tile_plan(key)[0]


def draw_tile_row(key, part):
    return tile_plan(key)[1]


def draw_owner_slot(key, part):
    return tile_plan(key)[2]


def block_levels(stream_key, dims, pieces, smallest, high):
    def one(axis_at, parts):
        steps = jax.random.uniform(jax.random.fold_in(jax.random.fold_in(stream_key, 6), axis_at), (parts,), jnp.float32, smallest / len(pieces), high / len(pieces))
        return jnp.repeat(jnp.exp(steps), dims[axis_at] // parts).reshape((-1,) + (1,) * (len(dims) - axis_at - 1))

    loudness = one(*pieces[0])
    for cut in pieces[1:]:
        loudness = loudness * one(*cut)
    return loudness


def bell_draw(key, dims, scale, most, cuts=(), kind=jnp.bfloat16):
    loudness = block_levels(key, dims, cuts, -0.22, 0.18) if cuts else 1.0
    values = jax.random.normal(key, dims, jnp.float32) * scale * loudness
    return jnp.minimum(jnp.maximum(values, -most), most).astype(kind)


def setup_inputs(seed: int = 0) -> dict:
    key_list = jax.random.split(jax.random.key(seed), 16)
    image_center = bell_draw(key_list[0], (IMG_H, C, IMG_W), 1.0, 6.0, ((0, 32), (2, 16)))
    image_radius = jnp.clip(jnp.exp(math.log(4.982948303222656e-05) - 2.303782 * jax.random.uniform(key_list[1], (IMG_H, C, IMG_W), jnp.float32) ** block_levels(key_list[1], (IMG_H, C, IMG_W), ((0, 32), (2, 16)), -0.2, 0.2)), 4.976987838745117e-06, 4.982948303222656e-05).astype(jnp.bfloat16)
    first_kernel = bell_draw(key_list[2], (3, 3, C, C), (9 * C) ** -0.5, 0.125)
    first_bias = bell_draw(key_list[3], (C,), 0.5, 3.0, (), jnp.float32)
    second_kernel = bell_draw(key_list[4], (3, 3, C, C), (9 * C) ** -0.5, 0.125)
    second_bias = bell_draw(key_list[5], (C,), 0.5, 3.0, (), jnp.float32)
    third_weight = bell_draw(key_list[6], (C, C), C ** -0.5, 0.375)
    third_bias = bell_draw(key_list[7], (C,), 0.5, 3.0, (), jnp.float32)
    fourth_weight = bell_draw(key_list[8], (C, C), C ** -0.5, 0.375)
    fourth_bias = bell_draw(key_list[9], (C,), 0.5, 3.0, (), jnp.float32)
    score_weight = bell_draw(key_list[10], (C,), C ** -0.5, 0.375)
    score_bias = bell_draw(key_list[11], (1,), 1.0, 3.0, (), jnp.float32)
    tile_count = draw_tile_count(jax.random.fold_in(key_list[15], 71), 0)
    tile_row = draw_tile_row(jax.random.fold_in(key_list[15], 71), 0)
    owner_slot = draw_owner_slot(jax.random.fold_in(key_list[15], 71), 0)
    return {"image_center": image_center, "image_radius": image_radius, "first_kernel": first_kernel, "first_bias": first_bias, "second_kernel": second_kernel, "second_bias": second_bias, "third_weight": third_weight, "third_bias": third_bias, "fourth_weight": fourth_weight, "fourth_bias": fourth_bias, "score_weight": score_weight, "score_bias": score_bias, "tile_count": tile_count, "tile_row": tile_row, "owner_slot": owner_slot}


EPSILON = 1e-6


def interval_relu(center, radius):
    lower = jax.nn.relu(center - radius)
    upper = jax.nn.relu(center + radius)
    return ((lower + upper) * 0.5).astype(jnp.bfloat16), ((upper - lower) * 0.5).astype(jnp.bfloat16)


def relax_slopes(center, radius):
    upper = jax.nn.relu(center + radius)
    below = jax.nn.relu(radius - center)
    slope = upper / (upper + below + EPSILON)
    return slope.astype(jnp.bfloat16), (slope * below).astype(jnp.bfloat16)


def conv_layer(middle, radius, kernel, layer_bias):
    row_count = middle.shape[0]
    col_count = middle.shape[2]
    padded_mid = jnp.pad(middle.astype(jnp.float32), ((1, 1), (0, 0), (1, 1)))
    padded_rad = jnp.pad(radius.astype(jnp.float32), ((1, 1), (0, 0), (1, 1)))
    kernel_f = kernel.astype(jnp.float32)
    center = jnp.zeros(middle.shape, jnp.float32)
    spread = jnp.zeros(middle.shape, jnp.float32)
    for row_shift in range(3):
        for col_shift in range(3):
            window_mid = padded_mid[row_shift:row_shift + row_count, :, col_shift:col_shift + col_count]
            window_rad = padded_rad[row_shift:row_shift + row_count, :, col_shift:col_shift + col_count]
            center = center + jnp.einsum("oi,riw->row", kernel_f[row_shift, col_shift], window_mid)
            spread = spread + jnp.einsum("oi,riw->row", jnp.abs(kernel_f[row_shift, col_shift]), window_rad)
    return center + layer_bias[None, :, None], spread


def head_layer(middle, radius, weight, layer_bias):
    weight_f = weight.astype(jnp.float32)
    center = jnp.einsum("oi,riw->row", weight_f, middle.astype(jnp.float32)) + layer_bias[None, :, None]
    spread = jnp.einsum("oi,riw->row", jnp.abs(weight_f), radius.astype(jnp.float32))
    return center, spread


def backward_bounds(tiles, third_weight, third_bias, fourth_weight, fourth_bias, score_weight):
    signs = jnp.array([1.0, -1.0], jnp.float32)
    slope_three = tiles[:, 0].astype(jnp.float32)
    offset_three = tiles[:, 1].astype(jnp.float32)
    slope_four = tiles[:, 2].astype(jnp.float32)
    offset_four = tiles[:, 3].astype(jnp.float32)
    middle_two = tiles[:, 4].astype(jnp.float32)
    radius_two = tiles[:, 5].astype(jnp.float32)
    direction = signs[:, None] * score_weight.astype(jnp.float32)[None, :]
    coeff_four = (direction[:, None, :, None] * slope_four[None]).astype(jnp.bfloat16)
    constant = jnp.sum(jnp.minimum(direction, 0.0)[:, None, :, None] * offset_four[None]
                       + coeff_four.astype(jnp.float32) * fourth_bias[None, None, :, None], axis=2)
    carried = jnp.einsum("sjcp,cd->sjdp", coeff_four.astype(jnp.float32), fourth_weight.astype(jnp.float32))
    coeff_three = (carried * slope_three[None]).astype(jnp.bfloat16)
    constant = constant + jnp.sum(jnp.minimum(carried, 0.0) * offset_three[None]
                                  + coeff_three.astype(jnp.float32) * third_bias[None, None, :, None], axis=2)
    reached = jnp.einsum("sjcp,cd->sjdp", coeff_three.astype(jnp.float32), third_weight.astype(jnp.float32))
    constant = constant + jnp.sum(reached * middle_two[None] - jnp.abs(reached) * radius_two[None], axis=2)
    return constant


def reference(image_center, image_radius, first_kernel, first_bias, second_kernel, second_bias,
              third_weight, third_bias, fourth_weight, fourth_bias, score_weight, score_bias,
              tile_count, tile_row, owner_slot):
    middle_one, radius_one = interval_relu(*conv_layer(image_center, image_radius, first_kernel, first_bias))
    middle_two, radius_two = interval_relu(*conv_layer(middle_one, radius_one, second_kernel, second_bias))
    pre_three = head_layer(middle_two, radius_two, third_weight, third_bias)
    slope_three, offset_three = relax_slopes(*pre_three)
    middle_three, radius_three = interval_relu(*pre_three)
    pre_four = head_layer(middle_three, radius_three, fourth_weight, fourth_bias)
    slope_four, offset_four = relax_slopes(*pre_four)
    middle_four, radius_four = interval_relu(*pre_four)
    score_f = score_weight.astype(jnp.float32)
    score_center = jnp.einsum("c,rcw->rw", score_f, middle_four.astype(jnp.float32)) + score_bias[0]
    score_radius = jnp.einsum("c,rcw->rw", jnp.abs(score_f), radius_four.astype(jnp.float32))
    ibp_bounds = jnp.stack([score_center - score_radius, score_center + score_radius])
    stacked = jnp.stack([slope_three, offset_three, slope_four, offset_four, middle_two, radius_two], axis=1)
    blocks = stacked.reshape(IMG_H, 6, C, N_CHAN, PIX)
    slab_index = jnp.arange(N_SLAB, dtype=jnp.int32)[:, None, None]
    chan_index = jnp.arange(N_CHAN, dtype=jnp.int32)[None, :, None]
    rows_global = (slab_index * ROWS_DEV + tile_row).astype(jnp.int32)
    tiles = blocks[rows_global, :, :, chan_index, :]
    tiles = tiles.reshape(N_SLAB * N_CHAN * TILES_DEV, 6, C, PIX)
    lowest = backward_bounds(tiles, third_weight, third_bias, fourth_weight, fourth_bias, score_weight)
    signs = jnp.array([1.0, -1.0], jnp.float32)
    lowest = lowest + signs[:, None, None] * score_bias[0]
    bounds = jnp.stack([lowest[0], -lowest[1]], axis=1)
    present = jnp.arange(TILES_DEV, dtype=jnp.int32)[None, None, :] < tile_count[:, :, None]
    target = jnp.where(present, owner_slot, N_SLAB * SLOT_CAP).reshape(-1).astype(jnp.int32)
    refined = jnp.zeros((N_SLAB * SLOT_CAP, 2, PIX), jnp.float32).at[target].set(bounds, mode="drop")
    return ibp_bounds, refined
```

```python
import functools

import jax
import jax.numpy as jnp
from jax import lax
from jax.experimental import pallas as pl
from jax.experimental.pallas import tpu as pltpu
from jax.sharding import PartitionSpec as P

EPSILON = 1e-06
MESH = pl.DeviceIdType.MESH
BF = jnp.bfloat16
F32 = jnp.float32
C = 256
PIX = 128
ROWS = 8
PAD = 144


def dot_nt(lhs, rhs):
    return lax.dot_general(lhs, rhs, (((1,), (1,)), ((), ())), preferred_element_type=F32)


def dot_nn(lhs, rhs):
    return lax.dot_general(lhs, rhs, (((1,), (0,)), ((), ())), preferred_element_type=F32)


def interval_relu(center, radius):
    lower = jnp.maximum(center - radius, 0.0)
    upper = jnp.maximum(center + radius, 0.0)
    return (lower + upper) * 0.5, (upper - lower) * 0.5


def relax_slopes(center, radius):
    upper = jnp.maximum(center + radius, 0.0)
    below = jnp.maximum(radius - center, 0.0)
    slope = upper / (upper + below + EPSILON)
    return slope.astype(BF).astype(F32), (slope * below).astype(BF).astype(F32)


def kernel(
    n_slab,
    n_chan,
    center_in,
    radius_in,
    first_in,
    second_in,
    third_in,
    fourth_in,
    first_bias,
    second_bias,
    third_bias,
    fourth_bias,
    score_weight,
    score_bias,
    tile_count,
    tile_row,
    owner_slot,
    ibp_out,
    refined_out,
    raw,
    wide,
    side,
    layer,
    first,
    second,
    third,
    fourth,
    gathered,
    message,
    arrived,
    local_sem,
    halo_send,
    halo_recv,
    chan_send,
    chan_recv,
    slab_send,
    slab_recv,
):
    s = lax.axis_index("slab")
    c = lax.axis_index("chan")

    def slab_at(step):
        return lax.rem(s + step + n_slab, n_slab)

    def chan_at(step):
        return lax.rem(c + step + n_chan, n_chan)

    loads = [
        pltpu.make_async_copy(center_in, raw.at[0, pl.ds(2, ROWS)], local_sem.at[0]),
        pltpu.make_async_copy(radius_in, raw.at[1, pl.ds(2, ROWS)], local_sem.at[1]),
        pltpu.make_async_copy(first_in, first, local_sem.at[2]),
        pltpu.make_async_copy(second_in, second, local_sem.at[3]),
        pltpu.make_async_copy(third_in, third, local_sem.at[4]),
        pltpu.make_async_copy(fourth_in, fourth, local_sem.at[5]),
    ]
    for load in loads:
        load.start()

    barrier = pltpu.get_barrier_semaphore()

    def greet_chan(step, carry):
        pl.semaphore_signal(
            barrier, inc=1, device_id=(s, chan_at(step)), device_id_type=MESH
        )
        return carry

    def greet_slab(step, carry):
        pl.semaphore_signal(
            barrier, inc=1, device_id=(slab_at(step), c), device_id_type=MESH
        )
        return carry

    for row_step in (-1, 1):
        for col_step in (-1, 1):
            pl.semaphore_signal(
                barrier,
                inc=1,
                device_id=(slab_at(row_step), chan_at(col_step)),
                device_id_type=MESH,
            )
    lax.fori_loop(1, n_chan, greet_chan, 0)
    lax.fori_loop(1, n_slab, greet_slab, 0)
    pl.semaphore_wait(barrier, n_chan + n_slab + 2)

    def send(index, source, target, row_step, col_step):
        copy = pltpu.make_async_remote_copy(
            src_ref=source,
            dst_ref=target,
            send_sem=halo_send.at[index],
            recv_sem=halo_recv.at[index],
            device_id=(slab_at(row_step), chan_at(col_step)),
            device_id_type=MESH,
        )
        copy.start()
        return copy

    row_copies = [
        send(0, center_in.at[pl.ds(6, 2)], raw.at[0, pl.ds(0, 2)], 1, 0),
        send(1, center_in.at[pl.ds(0, 2)], raw.at[0, pl.ds(10, 2)], -1, 0),
        send(2, radius_in.at[pl.ds(6, 2)], raw.at[1, pl.ds(0, 2)], 1, 0),
        send(3, radius_in.at[pl.ds(0, 2)], raw.at[1, pl.ds(10, 2)], -1, 0),
    ]

    place = lax.broadcasted_iota(jnp.int32, (3, PAD, PIX), 1)
    shift = lax.broadcasted_iota(jnp.int32, (3, PAD, PIX), 0)
    column = lax.broadcasted_iota(jnp.int32, (3, PAD, PIX), 2)
    select = jnp.where(place - 9 + shift == column, 1.0, 0.0).astype(BF)
    select = select.reshape(3 * PAD, PIX)

    def widen(kind, row, scale):
        turned = dot_nt(select, raw[kind, row])
        if scale is not None:
            turned = turned * scale
        turned = turned.astype(BF)
        for offset in range(3):
            wide[offset, kind, row] = turned[offset * PAD : (offset + 1) * PAD]

    loads[0].wait()
    loads[1].wait()

    def widen_own(row, carry):
        widen(0, row + 2, None)
        widen(1, row + 2, None)
        return carry

    lax.fori_loop(0, ROWS, widen_own, 0)

    last = pl.ds(PIX, 16)
    early = pl.ds(0, 16)
    own = pl.ds(2, ROWS)
    side_copies = [
        send(4, wide.at[1, :, own, last], side.at[0, :, own], 0, 1),
        send(5, wide.at[1, :, own, early], side.at[1, :, own], 0, -1),
        send(6, wide.at[1, :, pl.ds(8, 2), last], side.at[0, :, pl.ds(0, 2)], 1, 1),
        send(7, wide.at[1, :, pl.ds(8, 2), early], side.at[1, :, pl.ds(0, 2)], 1, -1),
        send(8, wide.at[1, :, pl.ds(2, 2), last], side.at[0, :, pl.ds(10, 2)], -1, 1),
        send(9, wide.at[1, :, pl.ds(2, 2), early], side.at[1, :, pl.ds(10, 2)], -1, -1),
    ]

    above = jnp.where(s > 0, 1.0, 0.0).astype(F32)
    below = jnp.where(s < n_slab - 1, 1.0, 0.0).astype(F32)
    leftward = jnp.where(c > 0, 1.0, 0.0).astype(F32)
    rightward = jnp.where(c < n_chan - 1, 1.0, 0.0).astype(F32)

    for copy in row_copies:
        copy.wait()

    def widen_halo(kind, carry):
        for row in (0, 1):
            widen(kind, row, above)
        for row in (10, 11):
            widen(kind, row, below)
        return carry

    lax.fori_loop(0, 2, widen_halo, 0)

    for copy in side_copies:
        copy.wait()
    lane_row = lax.broadcasted_iota(jnp.int32, (16, C), 0)
    edge = (lane_row == 7) | (lane_row == 8)

    def patch(row, carry):
        inside = jnp.where(row < 2, above, jnp.where(row > 9, below, 1.0))
        for kind in range(2):
            low = side[0, kind, row].astype(F32) * (inside * leftward)
            high = side[1, kind, row].astype(F32) * (inside * rightward)
            tile = wide[1, kind, row, 0:16].astype(F32)
            wide[1, kind, row, 0:16] = jnp.where(lane_row < 8, low, tile).astype(BF)
            tile = wide[0, kind, row, 0:16].astype(F32)
            wide[0, kind, row, 0:16] = jnp.where(edge, pltpu.roll(low, 1, 0), tile).astype(BF)
            tile = wide[1, kind, row, PIX:PAD].astype(F32)
            wide[1, kind, row, PIX:PAD] = jnp.where(lane_row >= 8, high, tile).astype(BF)
            tile = wide[2, kind, row, PIX:PAD].astype(F32)
            wide[2, kind, row, PIX:PAD] = jnp.where(edge, pltpu.roll(high, 15, 0), tile).astype(BF)
        return carry

    lax.fori_loop(0, ROWS + 4, patch, 0)

    loads[2].wait()
    n1 = 5

    def layer_one(part, carry):
        base = part * n1
        center = jnp.zeros((n1 * PAD, C), F32)
        radius = jnp.zeros((n1 * PAD, C), F32)
        for a in range(3):
            for b in range(3):
                weight = first[a, b]
                mid_in = wide[b, 0, pl.ds(base + a, n1)].reshape(n1 * PAD, C)
                rad_in = wide[b, 1, pl.ds(base + a, n1)].reshape(n1 * PAD, C)
                center = center + dot_nt(mid_in, weight)
                radius = radius + dot_nt(rad_in, jnp.abs(weight))
        middle, spread = interval_relu(center + first_bias[...], radius)
        row_at = lax.broadcasted_iota(jnp.int32, (n1, PAD, C), 0) + base + (s * ROWS - 1)
        col_at = lax.broadcasted_iota(jnp.int32, (n1, PAD, C), 1) + (c * PIX - 8)
        inside = (
            (row_at >= 0)
            & (row_at < n_slab * ROWS)
            & (col_at >= 0)
            & (col_at < n_chan * PIX)
        )
        middle = jnp.where(inside, middle.reshape(n1, PAD, C), 0.0)
        spread = jnp.where(inside, spread.reshape(n1, PAD, C), 0.0)
        for b in range(3):
            layer[b, 0, pl.ds(base, n1)] = middle[:, 7 + b : 7 + b + PIX].astype(BF)
            layer[b, 1, pl.ds(base, n1)] = spread[:, 7 + b : 7 + b + PIX].astype(BF)
        return carry

    lax.fori_loop(0, 2, layer_one, 0)

    for load in loads[3:]:
        load.wait()

    def layer_two(read, count):
        center = jnp.zeros((count * PIX, C), F32)
        radius = jnp.zeros((count * PIX, C), F32)
        for a in range(3):
            for b in range(3):
                weight = second[a, b]
                center = center + dot_nt(read(b, 0, a), weight)
                radius = radius + dot_nt(read(b, 1, a), jnp.abs(weight))
        middle, spread = interval_relu(center + second_bias[...], radius)
        return middle.astype(BF), spread.astype(BF)

    def head(middle, spread, weight, bias):
        return dot_nt(middle, weight) + bias, dot_nt(spread, jnp.abs(weight))

    first_row = tile_row[0, 0]
    second_row = tile_row[0, 1]

    def read_tiles(b, kind, a):
        return jnp.concatenate(
            [layer[b, kind, first_row + a], layer[b, kind, second_row + a]], axis=0
        )

    middle_two, radius_two = layer_two(read_tiles, 2)
    pre_three = head(middle_two, radius_two, third[...], third_bias[...])
    slope_three, offset_three = relax_slopes(*pre_three)
    middle_three, radius_three = interval_relu(*pre_three)
    pre_four = head(
        middle_three.astype(BF), radius_three.astype(BF), fourth[...], fourth_bias[...]
    )
    slope_four, offset_four = relax_slopes(*pre_four)
    score = score_weight[...].astype(F32)
    coeff_four = (score * slope_four).astype(BF)
    carried = dot_nn(coeff_four, fourth[...])
    coeff_three = (carried * slope_three).astype(BF)
    reached = dot_nn(coeff_three, third[...])
    shared = (
        coeff_four.astype(F32) * fourth_bias[...]
        + coeff_three.astype(F32) * third_bias[...]
        + reached * middle_two.astype(F32)
    )
    reach = jnp.abs(reached) * radius_two.astype(F32)
    lower = (
        shared + jnp.minimum(score, 0.0) * offset_four + jnp.minimum(carried, 0.0) * offset_three
    ) - reach
    upper = (
        shared + jnp.maximum(score, 0.0) * offset_four + jnp.maximum(carried, 0.0) * offset_three
    ) + reach
    bias_score = score_bias[0, 0]

    def column_sum(value):
        halves = value[:, :PIX] + value[:, PIX:]
        return jnp.sum(halves.T, axis=0, keepdims=True) + bias_score

    sub = lax.broadcasted_iota(jnp.int32, (8, PIX), 0)
    blob = jnp.zeros((8, PIX), F32)
    for tile in range(2):
        rows = slice(tile * PIX, (tile + 1) * PIX)
        blob = jnp.where(sub == 2 * tile, column_sum(lower[rows]), blob)
        blob = jnp.where(sub == 2 * tile + 1, column_sum(upper[rows]), blob)
        slot = jnp.where(tile < tile_count[0, 0], owner_slot[0, tile], -1)
        blob = jnp.where(sub == 4 + tile, slot.astype(F32), blob)
    gathered[c] = blob

    def chan_copy(step):
        return pltpu.make_async_remote_copy(
            src_ref=gathered.at[c],
            dst_ref=gathered.at[c],
            send_sem=chan_send.at[step - 1],
            recv_sem=chan_recv.at[step - 1],
            device_id=(s, chan_at(step)),
            device_id_type=MESH,
        )

    def chan_start(step, carry):
        chan_copy(step).start()
        return carry

    def chan_wait(step, carry):
        chan_copy(step).wait()
        return carry

    lax.fori_loop(1, n_chan, chan_start, 0)

    n2 = 4
    score_rows = jnp.broadcast_to(score_weight[...], (16, C)).astype(BF)

    def forward(part):
        def read(b, kind, a):
            return layer[b, kind, pl.ds(part * n2 + a, n2)].reshape(n2 * PIX, C)

        middle, spread = layer_two(read, n2)
        middle, spread = interval_relu(*head(middle, spread, third[...], third_bias[...]))
        middle, spread = interval_relu(
            *head(middle.astype(BF), spread.astype(BF), fourth[...], fourth_bias[...])
        )
        center = dot_nt(score_rows, middle.astype(BF)) + bias_score
        radius = dot_nt(jnp.abs(score_rows), spread.astype(BF))
        low = (center - radius)[:8]
        high = (center + radius)[:8]
        for row in range(n2):
            cols = slice(row * PIX, (row + 1) * PIX)
            ibp_out[0, pl.ds(part * n2 + row, 1)] = low[0:1, cols]
            ibp_out[1, pl.ds(part * n2 + row, 1)] = high[0:1, cols]

    forward(0)

    lax.fori_loop(1, n_chan, chan_wait, 0)
    keeper = lax.broadcasted_iota(jnp.int32, (n_slab, PIX), 0).astype(F32) * 8.0

    def collect(peer, carry):
        low, high, slots = carry
        for tile in range(2):
            slot = gathered[peer, 4 + tile : 5 + tile]
            mine = (slot >= keeper) & (slot < keeper + 8.0)
            low = jnp.where(mine, gathered[peer, 2 * tile : 2 * tile + 1], low)
            high = jnp.where(mine, gathered[peer, 2 * tile + 1 : 2 * tile + 2], high)
            slots = jnp.where(mine, slot - keeper + 1.0, slots)
        return low, high, slots

    empty = jnp.zeros((n_slab, PIX), F32)
    low, high, slots = lax.fori_loop(0, n_chan, collect, (empty, empty, empty))
    message[:, 0, :] = low
    message[:, 1, :] = high
    message[:, 2, :] = slots
    arrived[s] = message[s]

    def slab_copy(step):
        return pltpu.make_async_remote_copy(
            src_ref=message.at[slab_at(step)],
            dst_ref=arrived.at[s],
            send_sem=slab_send.at[step - 1],
            recv_sem=slab_recv.at[step - 1],
            device_id=(slab_at(step), c),
            device_id_type=MESH,
        )

    def slab_start(step, carry):
        slab_copy(step).start()
        return carry

    def slab_wait(step, carry):
        slab_copy(step).wait()
        return carry

    lax.fori_loop(1, n_slab, slab_start, 0)

    forward(1)

    lax.fori_loop(1, n_slab, slab_wait, 0)
    wanted = lax.broadcasted_iota(jnp.int32, (8, PIX), 0).astype(F32) + 1.0

    def keep(peer, carry):
        low, high = carry
        mine = arrived[peer, 2:3] == wanted
        return (
            jnp.where(mine, arrived[peer, 0:1], low),
            jnp.where(mine, arrived[peer, 1:2], high),
        )

    empty = jnp.zeros((8, PIX), F32)
    low, high = lax.fori_loop(0, n_slab, keep, (empty, empty))
    refined_out[:, 0, :] = low
    refined_out[:, 1, :] = high


def solution(mesh):
    n_slab = mesh.shape["slab"]
    n_chan = mesh.shape["chan"]

    def body(
        image_center,
        image_radius,
        first_kernel,
        first_bias,
        second_kernel,
        second_bias,
        third_weight,
        third_bias,
        fourth_weight,
        fourth_bias,
        score_weight,
        score_bias,
        tile_count,
        tile_row,
        owner_slot,
    ):
        hbm = pl.BlockSpec(memory_space=pl.ANY)
        vmem = pl.BlockSpec(memory_space=pltpu.VMEM)
        smem = pl.BlockSpec(memory_space=pltpu.SMEM)
        dma = pltpu.SemaphoreType.DMA
        return pl.pallas_call(
            functools.partial(kernel, n_slab, n_chan),
            out_shape=(
                jax.ShapeDtypeStruct((2, ROWS, PIX), F32),
                jax.ShapeDtypeStruct((8, 2, PIX), F32),
            ),
            in_specs=[hbm] * 6 + [vmem] * 5 + [smem] * 4,
            out_specs=(vmem, vmem),
            scratch_shapes=[
                pltpu.VMEM((2, ROWS + 4, C, PIX), BF),
                pltpu.VMEM((3, 2, ROWS + 4, PAD, C), BF),
                pltpu.VMEM((2, 2, ROWS + 4, 16, C), BF),
                pltpu.VMEM((3, 2, ROWS + 2, PIX, C), BF),
                pltpu.VMEM((3, 3, C, C), BF),
                pltpu.VMEM((3, 3, C, C), BF),
                pltpu.VMEM((C, C), BF),
                pltpu.VMEM((C, C), BF),
                pltpu.VMEM((n_chan, 8, PIX), F32),
                pltpu.VMEM((n_slab, 3, PIX), F32),
                pltpu.VMEM((n_slab, 3, PIX), F32),
                dma((6,)),
                dma((10,)),
                dma((10,)),
                dma((n_chan - 1,)),
                dma((n_chan - 1,)),
                dma((n_slab - 1,)),
                dma((n_slab - 1,)),
            ],
            compiler_params=pltpu.CompilerParams(
                collective_id=0, has_side_effects=True, vmem_limit_bytes=56 * 1024 * 1024
            ),
        )(
            image_center,
            image_radius,
            first_kernel,
            second_kernel,
            third_weight,
            fourth_weight,
            first_bias[None, :],
            second_bias[None, :],
            third_bias[None, :],
            fourth_bias[None, :],
            score_weight[None, :],
            score_bias[None, :],
            tile_count,
            tile_row[0],
            owner_slot[0],
        )

    placed = (
        P("slab", None, "chan"),
        P("slab", None, "chan"),
        *(P(),) * 10,
        P("slab", "chan"),
        P("slab", "chan", None),
        P("slab", "chan", None),
    )
    return jax.shard_map(
        body,
        mesh=mesh,
        in_specs=placed,
        out_specs=(P(None, "slab", "chan"), P("slab", None, None)),
        check_vma=False,
    )
```

```python
import functools

import jax
import jax.numpy as jnp
from jax import lax
from jax.experimental import pallas as pl
from jax.experimental.pallas import tpu as pltpu
from jax.sharding import PartitionSpec as P

EPSILON = 1e-06
MESH = pl.DeviceIdType.MESH
BF = jnp.bfloat16
F32 = jnp.float32
C = 256
PIX = 128
ROWS = 8
PAD = 144


def dot_nt(lhs, rhs):
    return lax.dot_general(lhs, rhs, (((1,), (1,)), ((), ())), preferred_element_type=F32)


def dot_nn(lhs, rhs):
    return lax.dot_general(lhs, rhs, (((1,), (0,)), ((), ())), preferred_element_type=F32)


def interval_relu(center, radius):
    lower = jnp.maximum(center - radius, 0.0)
    upper = jnp.maximum(center + radius, 0.0)
    return (lower + upper) * 0.5, (upper - lower) * 0.5


def relax_slopes(center, radius):
    upper = jnp.maximum(center + radius, 0.0)
    below = jnp.maximum(radius - center, 0.0)
    slope = upper / (upper + below + EPSILON)
    return slope.astype(BF).astype(F32), (slope * below).astype(BF).astype(F32)


def kernel(
    n_slab,
    n_chan,
    center_in,
    radius_in,
    first_in,
    second_in,
    third_in,
    fourth_in,
    first_bias,
    second_bias,
    third_bias,
    fourth_bias,
    score_weight,
    score_bias,
    tile_count,
    tile_row,
    owner_slot,
    out,
    raw,
    wide,
    edges,
    side,
    layer,
    first,
    second,
    third,
    fourth,
    gathered,
    message,
    arrived,
    local_sem,
    halo_send,
    halo_recv,
    chan_send,
    chan_recv,
    slab_send,
    slab_recv,
):
    s = lax.axis_index("slab")
    c = lax.axis_index("chan")

    def slab_at(step):
        return lax.rem(s + step + n_slab, n_slab)

    def chan_at(step):
        return lax.rem(c + step + n_chan, n_chan)

    loads = [
        pltpu.make_async_copy(center_in, raw.at[0, pl.ds(2, ROWS)], local_sem.at[0]),
        pltpu.make_async_copy(radius_in, raw.at[1, pl.ds(2, ROWS)], local_sem.at[1]),
        pltpu.make_async_copy(first_in, first, local_sem.at[2]),
        pltpu.make_async_copy(second_in, second, local_sem.at[3]),
        pltpu.make_async_copy(third_in, third, local_sem.at[4]),
        pltpu.make_async_copy(fourth_in, fourth, local_sem.at[5]),
    ]
    for load in loads:
        load.start()

    barrier = pltpu.get_barrier_semaphore()

    def greet_chan(step, carry):
        pl.semaphore_signal(
            barrier, inc=1, device_id=(s, chan_at(step)), device_id_type=MESH
        )
        return carry

    def greet_slab(step, carry):
        pl.semaphore_signal(
            barrier, inc=1, device_id=(slab_at(step), c), device_id_type=MESH
        )
        return carry

    for row_step in (-1, 1):
        for col_step in (-1, 1):
            pl.semaphore_signal(
                barrier,
                inc=1,
                device_id=(slab_at(row_step), chan_at(col_step)),
                device_id_type=MESH,
            )
    lax.fori_loop(1, n_chan, greet_chan, 0)
    lax.fori_loop(1, n_slab, greet_slab, 0)

    def send(index, source, target, row_step, col_step):
        copy = pltpu.make_async_remote_copy(
            src_ref=source,
            dst_ref=target,
            send_sem=halo_send.at[index],
            recv_sem=halo_recv.at[index],
            device_id=(slab_at(row_step), chan_at(col_step)),
            device_id_type=MESH,
        )
        copy.start()
        return copy

    slot = lax.broadcasted_iota(jnp.int32, (32, PIX), 0)
    column = lax.broadcasted_iota(jnp.int32, (32, PIX), 1)
    outer = jnp.where(column < 2, column, jnp.where(column >= PIX - 2, column + 18 - PIX, 99))

    loads[0].wait()
    loads[1].wait()

    def pack(row, carry):
        pick = jnp.where(outer + 2 * row == slot, 1.0, 0.0).astype(BF)
        return tuple(
            total + dot_nt(pick, raw[kind, row + 2]) for kind, total in enumerate(carry)
        )

    empty = jnp.zeros((32, C), F32)
    packed = lax.fori_loop(0, ROWS, pack, (empty, empty))
    for kind in range(2):
        edges[0, kind] = packed[kind][:16].astype(BF)
        edges[1, kind] = packed[kind][16:].astype(BF)

    pl.semaphore_wait(barrier, n_chan + n_slab + 2)
    row_copies = [
        send(0, center_in.at[pl.ds(6, 2)], raw.at[0, pl.ds(0, 2)], 1, 0),
        send(1, center_in.at[pl.ds(0, 2)], raw.at[0, pl.ds(10, 2)], -1, 0),
        send(2, radius_in.at[pl.ds(6, 2)], raw.at[1, pl.ds(0, 2)], 1, 0),
        send(3, radius_in.at[pl.ds(0, 2)], raw.at[1, pl.ds(10, 2)], -1, 0),
    ]
    side_copies = [
        send(4, edges.at[1], side.at[0, 1], 0, 1),
        send(5, edges.at[0], side.at[1, 1], 0, -1),
    ]
    corner_copies = [
        send(6, edges.at[1], side.at[0, 0], 1, 1),
        send(7, edges.at[0], side.at[1, 0], 1, -1),
        send(8, edges.at[1], side.at[0, 2], -1, 1),
        send(9, edges.at[0], side.at[1, 2], -1, -1),
    ]

    place = lax.broadcasted_iota(jnp.int32, (3, PAD, PIX), 1)
    shift = lax.broadcasted_iota(jnp.int32, (3, PAD, PIX), 0)
    column = lax.broadcasted_iota(jnp.int32, (3, PAD, PIX), 2)
    select = jnp.where(place - 9 + shift == column, 1.0, 0.0).astype(BF)
    select = select.reshape(3 * PAD, PIX)

    def widen(kind, row, scale):
        turned = dot_nt(select, raw[kind, row])
        if scale is not None:
            turned = turned * scale
        turned = turned.astype(BF)
        for offset in range(3):
            wide[offset, kind, row] = turned[offset * PAD : (offset + 1) * PAD]

    def widen_own(row, carry):
        widen(0, row + 2, None)
        widen(1, row + 2, None)
        return carry

    lax.fori_loop(0, ROWS, widen_own, 0)

    above = jnp.where(s > 0, 1.0, 0.0).astype(F32)
    below = jnp.where(s < n_slab - 1, 1.0, 0.0).astype(F32)
    leftward = jnp.where(c > 0, 1.0, 0.0).astype(F32)
    rightward = jnp.where(c < n_chan - 1, 1.0, 0.0).astype(F32)

    line = lax.broadcasted_iota(jnp.int32, (16, C), 0)
    both = (line == 7) | (line == 8)

    def patch(row, group, line_at, scale):
        turn = 24 - 2 * line_at
        for kind in range(2):
            low = side[0, group, kind].astype(F32) * (scale * leftward)
            high = side[1, group, kind].astype(F32) * (scale * rightward)
            for offset, cols, mask, source, step in (
                (0, slice(0, 16), both, low, turn - 1),
                (1, slice(0, 16), line == 7, low, turn - 2),
                (1, slice(PIX, PAD), line == 8, high, turn),
                (2, slice(PIX, PAD), both, high, turn - 1),
            ):
                moved = pltpu.roll(source, step % 16, 0)
                tile = wide[offset, kind, row, cols].astype(F32)
                wide[offset, kind, row, cols] = jnp.where(mask, moved, tile).astype(BF)

    def patch_own(row, carry):
        patch(row + 2, 1, row, 1.0)
        return carry

    def layer_one(read, count, row_of):
        center = jnp.zeros((count * PAD, C), F32)
        radius = jnp.zeros((count * PAD, C), F32)
        for a in range(3):
            for b in range(3):
                weight = first[a, b]
                center = center + dot_nt(read(b, 0, a).reshape(count * PAD, C), weight)
                radius = radius + dot_nt(read(b, 1, a).reshape(count * PAD, C), jnp.abs(weight))
        middle, spread = interval_relu(center + first_bias[...], radius)
        row_at = row_of(lax.broadcasted_iota(jnp.int32, (count, PAD, C), 0)) + (s * ROWS - 1)
        col_at = lax.broadcasted_iota(jnp.int32, (count, PAD, C), 1) + (c * PIX - 8)
        inside = (
            (row_at >= 0)
            & (row_at < n_slab * ROWS)
            & (col_at >= 0)
            & (col_at < n_chan * PIX)
        )
        middle = jnp.where(inside, middle.reshape(count, PAD, C), 0.0)
        spread = jnp.where(inside, spread.reshape(count, PAD, C), 0.0)
        return middle, spread

    for copy in side_copies:
        copy.wait()
    lax.fori_loop(0, ROWS, patch_own, 0)
    loads[2].wait()

    inner = layer_one(lambda b, kind, a: wide[b, kind, 2 + a : 8 + a], 6, lambda row: row + 2)
    for kind in range(2):
        for b in range(3):
            layer[b, kind, 2:8] = inner[kind][:, 7 + b : 7 + b + PIX].astype(BF)

    for copy in row_copies + corner_copies:
        copy.wait()

    def widen_halo(kind, carry):
        for row in (0, 1):
            widen(kind, row, above)
        for row in (10, 11):
            widen(kind, row, below)
        return carry

    lax.fori_loop(0, 2, widen_halo, 0)

    def patch_halo(row, carry):
        patch(row, 0, row + 6, above)
        patch(row + 10, 2, row, below)
        return carry

    lax.fori_loop(0, 2, patch_halo, 0)
    outside = layer_one(
        lambda b, kind, a: jnp.concatenate(
            [wide[b, kind, a : a + 2], wide[b, kind, 8 + a : 10 + a]], axis=0
        ),
        4,
        lambda row: jnp.where(row < 2, row, row + 6),
    )
    for kind in range(2):
        for b in range(3):
            rows = outside[kind][:, 7 + b : 7 + b + PIX].astype(BF)
            layer[b, kind, 0:2] = rows[:2]
            layer[b, kind, 8:10] = rows[2:]

    for load in loads[3:]:
        load.wait()

    def layer_two(read, count):
        center = jnp.zeros((count * PIX, C), F32)
        radius = jnp.zeros((count * PIX, C), F32)
        for a in range(3):
            for b in range(3):
                weight = second[a, b]
                center = center + dot_nt(read(b, 0, a), weight)
                radius = radius + dot_nt(read(b, 1, a), jnp.abs(weight))
        middle, spread = interval_relu(center + second_bias[...], radius)
        return middle.astype(BF), spread.astype(BF)

    def head(middle, spread, weight, bias):
        return dot_nt(middle, weight) + bias, dot_nt(spread, jnp.abs(weight))

    first_row = tile_row[0, 0]
    second_row = tile_row[0, 1]

    def read_tiles(b, kind, a):
        return jnp.concatenate(
            [layer[b, kind, first_row + a], layer[b, kind, second_row + a]], axis=0
        )

    middle_two, radius_two = layer_two(read_tiles, 2)
    pre_three = head(middle_two, radius_two, third[...], third_bias[...])
    slope_three, offset_three = relax_slopes(*pre_three)
    middle_three, radius_three = interval_relu(*pre_three)
    pre_four = head(
        middle_three.astype(BF), radius_three.astype(BF), fourth[...], fourth_bias[...]
    )
    slope_four, offset_four = relax_slopes(*pre_four)
    score = score_weight[...].astype(F32).reshape(1, C)
    coeff_four = (score * slope_four).astype(BF)
    carried = dot_nn(coeff_four, fourth[...])
    coeff_three = (carried * slope_three).astype(BF)
    reached = dot_nn(coeff_three, third[...])
    shared = (
        coeff_four.astype(F32) * fourth_bias[...]
        + coeff_three.astype(F32) * third_bias[...]
        + reached * middle_two.astype(F32)
    )
    reach = jnp.abs(reached) * radius_two.astype(F32)
    lower = (
        shared + jnp.minimum(score, 0.0) * offset_four + jnp.minimum(carried, 0.0) * offset_three
    ) - reach
    upper = (
        shared + jnp.maximum(score, 0.0) * offset_four + jnp.maximum(carried, 0.0) * offset_three
    ) + reach
    bias_score = score_bias[0, 0]

    def column_sum(value):
        halves = value[:, :PIX] + value[:, PIX:]
        return jnp.sum(halves.T, axis=0, keepdims=True) + bias_score

    sub = lax.broadcasted_iota(jnp.int32, (8, PIX), 0)
    blob = jnp.zeros((8, PIX), F32)
    for tile in range(2):
        rows = slice(tile * PIX, (tile + 1) * PIX)
        blob = jnp.where(sub == 2 * tile, column_sum(lower[rows]), blob)
        blob = jnp.where(sub == 2 * tile + 1, column_sum(upper[rows]), blob)
        slot = jnp.where(tile < tile_count[0, 0], owner_slot[0, tile], -1)
        blob = jnp.where(sub == 4 + tile, slot.astype(F32), blob)
    gathered[c] = blob

    def chan_copy(step):
        return pltpu.make_async_remote_copy(
            src_ref=gathered.at[c],
            dst_ref=gathered.at[c],
            send_sem=chan_send.at[step - 1],
            recv_sem=chan_recv.at[step - 1],
            device_id=(s, chan_at(step)),
            device_id_type=MESH,
        )

    def chan_start(step, carry):
        chan_copy(step).start()
        return carry

    def chan_wait(step, carry):
        chan_copy(step).wait()
        return carry

    lax.fori_loop(1, n_chan, chan_start, 0)

    lax.fori_loop(1, n_chan, chan_wait, 0)
    keeper = lax.broadcasted_iota(jnp.int32, (n_slab, PIX), 0).astype(F32) * 8.0

    def collect(peer, carry):
        low, high, slots = carry
        for tile in range(2):
            slot = gathered[peer, 4 + tile : 5 + tile]
            mine = (slot >= keeper) & (slot < keeper + 8.0)
            low = jnp.where(mine, gathered[peer, 2 * tile : 2 * tile + 1], low)
            high = jnp.where(mine, gathered[peer, 2 * tile + 1 : 2 * tile + 2], high)
            slots = jnp.where(mine, slot - keeper + 1.0, slots)
        return low, high, slots

    empty = jnp.zeros((n_slab, PIX), F32)
    low, high, slots = lax.fori_loop(0, n_chan, collect, (empty, empty, empty))
    message[:, 0, :] = low
    message[:, 1, :] = high
    message[:, 2, :] = slots
    arrived[s] = message[s]

    def slab_copy(step):
        return pltpu.make_async_remote_copy(
            src_ref=message.at[slab_at(step)],
            dst_ref=arrived.at[s],
            send_sem=slab_send.at[step - 1],
            recv_sem=slab_recv.at[step - 1],
            device_id=(slab_at(step), c),
            device_id_type=MESH,
        )

    def slab_start(step, carry):
        slab_copy(step).start()
        return carry

    def slab_wait(step, carry):
        slab_copy(step).wait()
        return carry

    lax.fori_loop(1, n_slab, slab_start, 0)

    n2 = 4
    score_rows = jnp.broadcast_to(score, (16, C)).astype(BF)

    def forward(part, carry):
        def read(b, kind, a):
            return layer[b, kind, pl.ds(part * n2 + a, n2)].reshape(n2 * PIX, C)

        middle, spread = layer_two(read, n2)
        middle, spread = interval_relu(*head(middle, spread, third[...], third_bias[...]))
        middle, spread = interval_relu(
            *head(middle.astype(BF), spread.astype(BF), fourth[...], fourth_bias[...])
        )
        center = dot_nt(score_rows, middle.astype(BF)) + bias_score
        radius = dot_nt(jnp.abs(score_rows), spread.astype(BF))
        low = (center - radius)[:8]
        high = (center + radius)[:8]
        for row in range(n2):
            cols = slice(row * PIX, (row + 1) * PIX)
            out[pl.ds(part * n2 + row, 1)] = low[0:1, cols]
            out[pl.ds(ROWS + part * n2 + row, 1)] = high[0:1, cols]
        return carry

    lax.fori_loop(0, 2, forward, 0)

    lax.fori_loop(1, n_slab, slab_wait, 0)
    wanted = lax.broadcasted_iota(jnp.int32, (8, PIX), 0).astype(F32) + 1.0

    def keep(peer, carry):
        low, high = carry
        mine = arrived[peer, 2:3] == wanted
        return (
            jnp.where(mine, arrived[peer, 0:1], low),
            jnp.where(mine, arrived[peer, 1:2], high),
        )

    empty = jnp.zeros((8, PIX), F32)
    low, high = lax.fori_loop(0, n_slab, keep, (empty, empty))
    out[16:24] = low
    out[24:32] = high


def unpack(bounds, ibp_out, refined_out):
    ibp_out[0] = bounds[0:8]
    ibp_out[1] = bounds[8:16]
    refined_out[:, 0, :] = bounds[16:24]
    refined_out[:, 1, :] = bounds[24:32]


def solution(mesh):
    n_slab = mesh.shape["slab"]
    n_chan = mesh.shape["chan"]

    def body(
        image_center,
        image_radius,
        first_kernel,
        first_bias,
        second_kernel,
        second_bias,
        third_weight,
        third_bias,
        fourth_weight,
        fourth_bias,
        score_weight,
        score_bias,
        tile_count,
        tile_row,
        owner_slot,
    ):
        hbm = pl.BlockSpec(memory_space=pl.ANY)
        vmem = pl.BlockSpec(memory_space=pltpu.VMEM)
        smem = pl.BlockSpec(memory_space=pltpu.SMEM)
        dma = pltpu.SemaphoreType.DMA
        bounds = pl.pallas_call(
            functools.partial(kernel, n_slab, n_chan),
            out_shape=jax.ShapeDtypeStruct((32, PIX), F32),
            in_specs=[hbm] * 6 + [vmem] * 5 + [smem] * 4,
            out_specs=vmem,
            scratch_shapes=[
                pltpu.VMEM((2, ROWS + 4, C, PIX), BF),
                pltpu.VMEM((3, 2, ROWS + 4, PAD, C), BF),
                pltpu.VMEM((2, 2, 16, C), BF),
                pltpu.VMEM((2, 3, 2, 16, C), BF),
                pltpu.VMEM((3, 2, ROWS + 2, PIX, C), BF),
                pltpu.VMEM((3, 3, C, C), BF),
                pltpu.VMEM((3, 3, C, C), BF),
                pltpu.VMEM((C, C), BF),
                pltpu.VMEM((C, C), BF),
                pltpu.VMEM((n_chan, 8, PIX), F32),
                pltpu.VMEM((n_slab, 3, PIX), F32),
                pltpu.VMEM((n_slab, 3, PIX), F32),
                dma((6,)),
                dma((10,)),
                dma((10,)),
                dma((n_chan - 1,)),
                dma((n_chan - 1,)),
                dma((n_slab - 1,)),
                dma((n_slab - 1,)),
            ],
            compiler_params=pltpu.CompilerParams(
                collective_id=0, has_side_effects=True, vmem_limit_bytes=56 * 1024 * 1024
            ),
        )(
            image_center,
            image_radius,
            first_kernel,
            second_kernel,
            third_weight,
            fourth_weight,
            first_bias[None, :],
            second_bias[None, :],
            third_bias[None, :],
            fourth_bias[None, :],
            score_weight,
            score_bias[None, :],
            tile_count,
            tile_row[0],
            owner_slot[0],
        )
        return pl.pallas_call(
            unpack,
            out_shape=(
                jax.ShapeDtypeStruct((2, ROWS, PIX), F32),
                jax.ShapeDtypeStruct((8, 2, PIX), F32),
            ),
            in_specs=[vmem],
            out_specs=(vmem, vmem),
        )(bounds)

    placed = (
        P("slab", None, "chan"),
        P("slab", None, "chan"),
        *(P(),) * 10,
        P("slab", "chan"),
        P("slab", "chan", None),
        P("slab", "chan", None),
    )
    return jax.shard_map(
        body,
        mesh=mesh,
        in_specs=placed,
        out_specs=(P(None, "slab", "chan"), P("slab", None, None)),
        check_vma=False,
    )
```

```python
import functools

import jax
import jax.numpy as jnp
from jax import lax
from jax.experimental import pallas as pl
from jax.experimental.pallas import tpu as pltpu
from jax.sharding import PartitionSpec as P

EPSILON = 1e-06
MESH = pl.DeviceIdType.MESH
BF = jnp.bfloat16
F32 = jnp.float32
C = 256
PIX = 128
ROWS = 8
PAD = 144


def dot_nt(lhs, rhs):
    return lax.dot_general(lhs, rhs, (((1,), (1,)), ((), ())), preferred_element_type=F32)


def dot_nn(lhs, rhs):
    return lax.dot_general(lhs, rhs, (((1,), (0,)), ((), ())), preferred_element_type=F32)


def interval_relu(center, radius):
    lower = jnp.maximum(center - radius, 0.0)
    upper = jnp.maximum(center + radius, 0.0)
    return (lower + upper) * 0.5, (upper - lower) * 0.5


def relax_slopes(center, radius):
    upper = jnp.maximum(center + radius, 0.0)
    below = jnp.maximum(radius - center, 0.0)
    slope = upper / (upper + below + EPSILON)
    return slope.astype(BF).astype(F32), (slope * below).astype(BF).astype(F32)


def kernel(
    n_slab,
    n_chan,
    center_in,
    radius_in,
    first_in,
    second_in,
    third_in,
    fourth_in,
    first_bias,
    second_bias,
    third_bias,
    fourth_bias,
    score_weight,
    score_bias,
    tile_count,
    tile_row,
    owner_slot,
    out,
    raw,
    wide,
    edges,
    side,
    layer,
    first,
    second,
    third,
    fourth,
    gathered,
    message,
    arrived,
    local_sem,
    halo_send,
    halo_recv,
    chan_send,
    chan_recv,
    slab_send,
    slab_recv,
):
    s = lax.axis_index("slab")
    c = lax.axis_index("chan")

    def slab_at(step):
        return lax.rem(s + step + n_slab, n_slab)

    def chan_at(step):
        return lax.rem(c + step + n_chan, n_chan)

    loads = [
        pltpu.make_async_copy(center_in, raw.at[0, pl.ds(2, ROWS)], local_sem.at[0]),
        pltpu.make_async_copy(radius_in, raw.at[1, pl.ds(2, ROWS)], local_sem.at[1]),
        pltpu.make_async_copy(first_in, first, local_sem.at[2]),
        pltpu.make_async_copy(second_in, second, local_sem.at[3]),
        pltpu.make_async_copy(third_in, third, local_sem.at[4]),
        pltpu.make_async_copy(fourth_in, fourth, local_sem.at[5]),
    ]
    for load in loads:
        load.start()

    barrier = pltpu.get_barrier_semaphore()

    def greet(row_step, col_step):
        pl.semaphore_signal(
            barrier,
            inc=1,
            device_id=(slab_at(row_step), chan_at(col_step)),
            device_id_type=MESH,
        )

    for row_step in (-1, 1):
        for col_step in (-1, 1):
            greet(row_step, col_step)
    for step in range(1, n_chan):
        greet(0, step)
    for step in range(1, n_slab):
        greet(step, 0)

    def send(index, source, target, row_step, col_step):
        copy = pltpu.make_async_remote_copy(
            src_ref=source,
            dst_ref=target,
            send_sem=halo_send.at[index],
            recv_sem=halo_recv.at[index],
            device_id=(slab_at(row_step), chan_at(col_step)),
            device_id_type=MESH,
        )
        copy.start()
        return copy

    slot = lax.broadcasted_iota(jnp.int32, (32, PIX), 0)
    column = lax.broadcasted_iota(jnp.int32, (32, PIX), 1)
    outer = jnp.where(column < 2, column, jnp.where(column >= PIX - 2, column + 18 - PIX, 99))

    loads[0].wait()
    loads[1].wait()

    def pack(row, carry):
        pick = jnp.where(outer + 2 * row == slot, 1.0, 0.0).astype(BF)
        return tuple(
            total + dot_nt(pick, raw[kind, row + 2]) for kind, total in enumerate(carry)
        )

    empty = jnp.zeros((32, C), F32)
    packed = lax.fori_loop(0, ROWS, pack, (empty, empty))
    for kind in range(2):
        edges[0, kind] = packed[kind][:16].astype(BF)
        edges[1, kind] = packed[kind][16:].astype(BF)

    pl.semaphore_wait(barrier, n_chan + n_slab + 2)
    row_copies = [
        send(0, center_in.at[pl.ds(6, 2)], raw.at[0, pl.ds(0, 2)], 1, 0),
        send(1, center_in.at[pl.ds(0, 2)], raw.at[0, pl.ds(10, 2)], -1, 0),
        send(2, radius_in.at[pl.ds(6, 2)], raw.at[1, pl.ds(0, 2)], 1, 0),
        send(3, radius_in.at[pl.ds(0, 2)], raw.at[1, pl.ds(10, 2)], -1, 0),
    ]
    side_copies = [
        send(4, edges.at[1], side.at[0, 1], 0, 1),
        send(5, edges.at[0], side.at[1, 1], 0, -1),
    ]
    corner_copies = [
        send(6, edges.at[1], side.at[0, 0], 1, 1),
        send(7, edges.at[0], side.at[1, 0], 1, -1),
        send(8, edges.at[1], side.at[0, 2], -1, 1),
        send(9, edges.at[0], side.at[1, 2], -1, -1),
    ]

    place = lax.broadcasted_iota(jnp.int32, (3, PAD, PIX), 1)
    shift = lax.broadcasted_iota(jnp.int32, (3, PAD, PIX), 0)
    column = lax.broadcasted_iota(jnp.int32, (3, PAD, PIX), 2)
    select = jnp.where(place - 9 + shift == column, 1.0, 0.0).astype(BF)
    select = select.reshape(3 * PAD, PIX)

    def widen(kind, row, scale):
        turned = dot_nt(select, raw[kind, row])
        if scale is not None:
            turned = turned * scale
        turned = turned.astype(BF)
        for offset in range(3):
            wide[offset, kind, row] = turned[offset * PAD : (offset + 1) * PAD]

    def widen_own(row, carry):
        widen(0, row + 2, None)
        widen(1, row + 2, None)
        return carry

    lax.fori_loop(0, ROWS, widen_own, 0)

    above = jnp.where(s > 0, 1.0, 0.0).astype(F32)
    below = jnp.where(s < n_slab - 1, 1.0, 0.0).astype(F32)
    leftward = jnp.where(c > 0, 1.0, 0.0).astype(F32)
    rightward = jnp.where(c < n_chan - 1, 1.0, 0.0).astype(F32)

    line = lax.broadcasted_iota(jnp.int32, (16, C), 0)
    both = (line == 7) | (line == 8)

    def patch(row, group, line_at, scale):
        turn = 24 - 2 * line_at
        for kind in range(2):
            low = side[0, group, kind].astype(F32) * (scale * leftward)
            high = side[1, group, kind].astype(F32) * (scale * rightward)
            for offset, cols, mask, source, step in (
                (0, slice(0, 16), both, low, turn - 1),
                (1, slice(0, 16), line == 7, low, turn - 2),
                (1, slice(PIX, PAD), line == 8, high, turn),
                (2, slice(PIX, PAD), both, high, turn - 1),
            ):
                moved = pltpu.roll(source, step % 16, 0)
                tile = wide[offset, kind, row, cols].astype(F32)
                wide[offset, kind, row, cols] = jnp.where(mask, moved, tile).astype(BF)

    def patch_own(row, carry):
        patch(row + 2, 1, row, 1.0)
        return carry

    def layer_one(read, count, row_of):
        center = jnp.zeros((count * PAD, C), F32)
        radius = jnp.zeros((count * PAD, C), F32)
        for a in range(3):
            for b in range(3):
                weight = first[a, b]
                center = center + dot_nt(read(b, 0, a).reshape(count * PAD, C), weight)
                radius = radius + dot_nt(read(b, 1, a).reshape(count * PAD, C), jnp.abs(weight))
        middle, spread = interval_relu(center + first_bias[...], radius)
        row_at = row_of(lax.broadcasted_iota(jnp.int32, (count, PAD, C), 0)) + (s * ROWS - 1)
        col_at = lax.broadcasted_iota(jnp.int32, (count, PAD, C), 1) + (c * PIX - 8)
        inside = (
            (row_at >= 0)
            & (row_at < n_slab * ROWS)
            & (col_at >= 0)
            & (col_at < n_chan * PIX)
        )
        middle = jnp.where(inside, middle.reshape(count, PAD, C), 0.0)
        spread = jnp.where(inside, spread.reshape(count, PAD, C), 0.0)
        return middle, spread

    for copy in side_copies:
        copy.wait()
    lax.fori_loop(0, ROWS, patch_own, 0)
    loads[2].wait()

    inner = layer_one(lambda b, kind, a: wide[b, kind, 2 + a : 8 + a], 6, lambda row: row + 2)
    for kind in range(2):
        for b in range(3):
            layer[b, kind, 2:8] = inner[kind][:, 7 + b : 7 + b + PIX].astype(BF)

    for copy in row_copies + corner_copies:
        copy.wait()

    def widen_halo(kind, carry):
        for row in (0, 1):
            widen(kind, row, above)
        for row in (10, 11):
            widen(kind, row, below)
        return carry

    lax.fori_loop(0, 2, widen_halo, 0)

    def patch_halo(row, carry):
        patch(row, 0, row + 6, above)
        patch(row + 10, 2, row, below)
        return carry

    lax.fori_loop(0, 2, patch_halo, 0)
    outside = layer_one(
        lambda b, kind, a: jnp.concatenate(
            [wide[b, kind, a : a + 2], wide[b, kind, 8 + a : 10 + a]], axis=0
        ),
        4,
        lambda row: jnp.where(row < 2, row, row + 6),
    )
    for kind in range(2):
        for b in range(3):
            rows = outside[kind][:, 7 + b : 7 + b + PIX].astype(BF)
            layer[b, kind, 0:2] = rows[:2]
            layer[b, kind, 8:10] = rows[2:]

    for load in loads[3:]:
        load.wait()

    def layer_two(read, count):
        center = jnp.zeros((count * PIX, C), F32)
        radius = jnp.zeros((count * PIX, C), F32)
        for a in range(3):
            for b in range(3):
                weight = second[a, b]
                center = center + dot_nt(read(b, 0, a), weight)
                radius = radius + dot_nt(read(b, 1, a), jnp.abs(weight))
        middle, spread = interval_relu(center + second_bias[...], radius)
        return middle.astype(BF), spread.astype(BF)

    def head(middle, spread, weight, bias):
        return dot_nt(middle, weight) + bias, dot_nt(spread, jnp.abs(weight))

    first_row = tile_row[0, 0]
    second_row = tile_row[0, 1]

    def read_tiles(b, kind, a):
        return jnp.concatenate(
            [layer[b, kind, first_row + a], layer[b, kind, second_row + a]], axis=0
        )

    middle_two, radius_two = layer_two(read_tiles, 2)
    pre_three = head(middle_two, radius_two, third[...], third_bias[...])
    slope_three, offset_three = relax_slopes(*pre_three)
    middle_three, radius_three = interval_relu(*pre_three)
    pre_four = head(
        middle_three.astype(BF), radius_three.astype(BF), fourth[...], fourth_bias[...]
    )
    slope_four, offset_four = relax_slopes(*pre_four)
    score = score_weight[...].astype(F32).reshape(1, C)
    coeff_four = (score * slope_four).astype(BF)
    carried = dot_nn(coeff_four, fourth[...])
    coeff_three = (carried * slope_three).astype(BF)
    reached = dot_nn(coeff_three, third[...])
    shared = (
        coeff_four.astype(F32) * fourth_bias[...]
        + coeff_three.astype(F32) * third_bias[...]
        + reached * middle_two.astype(F32)
    )
    reach = jnp.abs(reached) * radius_two.astype(F32)
    lower = (
        shared + jnp.minimum(score, 0.0) * offset_four + jnp.minimum(carried, 0.0) * offset_three
    ) - reach
    upper = (
        shared + jnp.maximum(score, 0.0) * offset_four + jnp.maximum(carried, 0.0) * offset_three
    ) + reach
    bias_score = score_bias[0, 0]

    def column_sum(value):
        halves = value[:, :PIX] + value[:, PIX:]
        return jnp.sum(halves.T, axis=0, keepdims=True) + bias_score

    sub = lax.broadcasted_iota(jnp.int32, (8, PIX), 0)
    blob = jnp.zeros((8, PIX), F32)
    for tile in range(2):
        rows = slice(tile * PIX, (tile + 1) * PIX)
        blob = jnp.where(sub == 2 * tile, column_sum(lower[rows]), blob)
        blob = jnp.where(sub == 2 * tile + 1, column_sum(upper[rows]), blob)
        slot = jnp.where(tile < tile_count[0, 0], owner_slot[0, tile], -1)
        blob = jnp.where(sub == 4 + tile, slot.astype(F32), blob)
    gathered[c] = blob

    def chan_copy(step):
        return pltpu.make_async_remote_copy(
            src_ref=gathered.at[c],
            dst_ref=gathered.at[c],
            send_sem=chan_send.at[step - 1],
            recv_sem=chan_recv.at[step - 1],
            device_id=(s, chan_at(step)),
            device_id_type=MESH,
        )

    for step in range(1, n_chan):
        chan_copy(step).start()

    keeper = lax.broadcasted_iota(jnp.int32, (n_slab, PIX), 0).astype(F32) * 8.0

    def collect(peer, carry):
        low, high, slots = carry
        for tile in range(2):
            slot = gathered[peer, 4 + tile : 5 + tile]
            mine = (slot >= keeper) & (slot < keeper + 8.0)
            low = jnp.where(mine, gathered[peer, 2 * tile : 2 * tile + 1], low)
            high = jnp.where(mine, gathered[peer, 2 * tile + 1 : 2 * tile + 2], high)
            slots = jnp.where(mine, slot - keeper + 1.0, slots)
        return low, high, slots

    def collect_from(step, carry):
        chan_copy(step).wait_recv()
        return collect(chan_at(n_chan - step), carry)

    empty = jnp.zeros((n_slab, PIX), F32)
    found = collect(c, (empty, empty, empty))
    low, high, slots = lax.fori_loop(1, n_chan, collect_from, found)
    message[:, 0, :] = low
    message[:, 1, :] = high
    message[:, 2, :] = slots
    arrived[s] = message[s]

    def other(index):
        return index + lax.div(index - s + n_slab, n_slab)

    def slab_copy(index):
        return pltpu.make_async_remote_copy(
            src_ref=message.at[other(index)],
            dst_ref=arrived.at[s],
            send_sem=slab_send.at[index],
            recv_sem=slab_recv.at[s],
            device_id=(other(index), c),
            device_id_type=MESH,
        )

    def slab_arrival(index):
        return pltpu.make_async_remote_copy(
            src_ref=message.at[other(index)],
            dst_ref=arrived.at[other(index)],
            send_sem=slab_send.at[index],
            recv_sem=slab_recv.at[other(index)],
            device_id=(other(index), c),
            device_id_type=MESH,
        )

    for index in range(n_slab - 1):
        slab_copy(index).start()

    n2 = 4
    score_rows = jnp.broadcast_to(score, (16, C)).astype(BF)

    def forward(part, carry):
        def read(b, kind, a):
            return layer[b, kind, pl.ds(part * n2 + a, n2)].reshape(n2 * PIX, C)

        middle, spread = layer_two(read, n2)
        middle, spread = interval_relu(*head(middle, spread, third[...], third_bias[...]))
        middle, spread = interval_relu(
            *head(middle.astype(BF), spread.astype(BF), fourth[...], fourth_bias[...])
        )
        center = dot_nt(score_rows, middle.astype(BF)) + bias_score
        radius = dot_nt(jnp.abs(score_rows), spread.astype(BF))
        low = (center - radius)[:8]
        high = (center + radius)[:8]
        for row in range(n2):
            cols = slice(row * PIX, (row + 1) * PIX)
            out[pl.ds(part * n2 + row, 1)] = low[0:1, cols]
            out[pl.ds(ROWS + part * n2 + row, 1)] = high[0:1, cols]
        return carry

    lax.fori_loop(0, 2, forward, 0)

    wanted = lax.broadcasted_iota(jnp.int32, (8, PIX), 0).astype(F32) + 1.0

    def keep(peer, carry):
        low, high = carry
        mine = arrived[peer, 2:3] == wanted
        return (
            jnp.where(mine, arrived[peer, 0:1], low),
            jnp.where(mine, arrived[peer, 1:2], high),
        )

    empty = jnp.zeros((8, PIX), F32)

    def keep_from(index, carry):
        slab_arrival(index).wait_recv()
        return keep(other(index), carry)

    low, high = lax.fori_loop(0, n_slab - 1, keep_from, keep(s, (empty, empty)))
    out[16:24] = low
    out[24:32] = high

    def chan_sent(step, carry):
        chan_copy(step).wait_send()
        return carry

    def slab_sent(index, carry):
        slab_copy(index).wait_send()
        return carry

    lax.fori_loop(1, n_chan, chan_sent, 0)
    lax.fori_loop(0, n_slab - 1, slab_sent, 0)


def unpack(bounds, ibp_out, refined_out):
    ibp_out[0] = bounds[0:8]
    ibp_out[1] = bounds[8:16]
    refined_out[:, 0, :] = bounds[16:24]
    refined_out[:, 1, :] = bounds[24:32]


def solution(mesh):
    n_slab = mesh.shape["slab"]
    n_chan = mesh.shape["chan"]

    def body(
        image_center,
        image_radius,
        first_kernel,
        first_bias,
        second_kernel,
        second_bias,
        third_weight,
        third_bias,
        fourth_weight,
        fourth_bias,
        score_weight,
        score_bias,
        tile_count,
        tile_row,
        owner_slot,
    ):
        hbm = pl.BlockSpec(memory_space=pl.ANY)
        vmem = pl.BlockSpec(memory_space=pltpu.VMEM)
        smem = pl.BlockSpec(memory_space=pltpu.SMEM)
        dma = pltpu.SemaphoreType.DMA
        bounds = pl.pallas_call(
            functools.partial(kernel, n_slab, n_chan),
            out_shape=jax.ShapeDtypeStruct((32, PIX), F32),
            in_specs=[hbm] * 6 + [vmem] * 5 + [smem] * 4,
            out_specs=vmem,
            scratch_shapes=[
                pltpu.VMEM((2, ROWS + 4, C, PIX), BF),
                pltpu.VMEM((3, 2, ROWS + 4, PAD, C), BF),
                pltpu.VMEM((2, 2, 16, C), BF),
                pltpu.VMEM((2, 3, 2, 16, C), BF),
                pltpu.VMEM((3, 2, ROWS + 2, PIX, C), BF),
                pltpu.VMEM((3, 3, C, C), BF),
                pltpu.VMEM((3, 3, C, C), BF),
                pltpu.VMEM((C, C), BF),
                pltpu.VMEM((C, C), BF),
                pltpu.VMEM((n_chan, 8, PIX), F32),
                pltpu.VMEM((n_slab, 3, PIX), F32),
                pltpu.VMEM((n_slab, 3, PIX), F32),
                dma((6,)),
                dma((10,)),
                dma((10,)),
                dma((n_chan - 1,)),
                dma((n_chan - 1,)),
                dma((n_slab - 1,)),
                dma((n_slab,)),
            ],
            compiler_params=pltpu.CompilerParams(
                collective_id=0, has_side_effects=True, vmem_limit_bytes=56 * 1024 * 1024
            ),
        )(
            image_center,
            image_radius,
            first_kernel,
            second_kernel,
            third_weight,
            fourth_weight,
            first_bias[None, :],
            second_bias[None, :],
            third_bias[None, :],
            fourth_bias[None, :],
            score_weight,
            score_bias[None, :],
            tile_count,
            tile_row[0],
            owner_slot[0],
        )
        return pl.pallas_call(
            unpack,
            out_shape=(
                jax.ShapeDtypeStruct((2, ROWS, PIX), F32),
                jax.ShapeDtypeStruct((8, 2, PIX), F32),
            ),
            in_specs=[vmem],
            out_specs=(vmem, vmem),
        )(bounds)

    placed = (
        P("slab", None, "chan"),
        P("slab", None, "chan"),
        *(P(),) * 10,
        P("slab", "chan"),
        P("slab", "chan", None),
        P("slab", "chan", None),
    )
    return jax.shard_map(
        body,
        mesh=mesh,
        in_specs=placed,
        out_specs=(P(None, "slab", "chan"), P("slab", None, None)),
        check_vma=False,
    )
```

```python
import functools

import jax
import jax.numpy as jnp
from jax import lax
from jax.experimental import pallas as pl
from jax.experimental.pallas import tpu as pltpu
from jax.sharding import PartitionSpec as P

EPSILON = 1e-06
MESH = pl.DeviceIdType.MESH
BF = jnp.bfloat16
F32 = jnp.float32
C = 256
PIX = 128
ROWS = 8
PAD = 144


def dot_nt(lhs, rhs):
    return lax.dot_general(lhs, rhs, (((1,), (1,)), ((), ())), preferred_element_type=F32)


def dot_nn(lhs, rhs):
    return lax.dot_general(lhs, rhs, (((1,), (0,)), ((), ())), preferred_element_type=F32)


def interval_relu(center, radius):
    lower = jnp.maximum(center - radius, 0.0)
    upper = jnp.maximum(center + radius, 0.0)
    return (lower + upper) * 0.5, (upper - lower) * 0.5


def relax_slopes(center, radius):
    upper = jnp.maximum(center + radius, 0.0)
    below = jnp.maximum(radius - center, 0.0)
    slope = upper / (upper + below + EPSILON)
    return slope.astype(BF).astype(F32), (slope * below).astype(BF).astype(F32)


def kernel(
    n_slab,
    n_chan,
    center_in,
    radius_in,
    first_in,
    second_in,
    third_in,
    fourth_in,
    first_bias,
    second_bias,
    third_bias,
    fourth_bias,
    score_weight,
    score_bias,
    tile_count,
    tile_row,
    owner_slot,
    out,
    raw,
    wide,
    edges,
    side,
    layer,
    first,
    second,
    third,
    fourth,
    gathered,
    message,
    arrived,
    known,
    local_sem,
    halo_send,
    halo_recv,
    chan_send,
    chan_recv,
    slab_send,
    slab_recv,
):
    s = lax.axis_index("slab")
    c = lax.axis_index("chan")

    def slab_at(step):
        return lax.rem(s + step + n_slab, n_slab)

    def chan_at(step):
        return lax.rem(c + step + n_chan, n_chan)

    loads = [
        pltpu.make_async_copy(center_in, raw.at[0, pl.ds(2, ROWS)], local_sem.at[0]),
        pltpu.make_async_copy(radius_in, raw.at[1, pl.ds(2, ROWS)], local_sem.at[1]),
        pltpu.make_async_copy(first_in, first, local_sem.at[2]),
        pltpu.make_async_copy(second_in, second, local_sem.at[3]),
        pltpu.make_async_copy(third_in, third, local_sem.at[4]),
        pltpu.make_async_copy(fourth_in, fourth, local_sem.at[5]),
    ]
    for load in loads:
        load.start()

    barrier = pltpu.get_barrier_semaphore()

    def greet(row_step, col_step):
        pl.semaphore_signal(
            barrier,
            inc=1,
            device_id=(slab_at(row_step), chan_at(col_step)),
            device_id_type=MESH,
        )

    for row_step in (-1, 0, 1):
        for col_step in (-1, 0, 1):
            if row_step or col_step:
                greet(row_step, col_step)

    rounds = []
    distance = 1
    while 2 * distance < max(n_slab, n_chan):
        along = [(distance, 0), (-distance, 0)] if 2 * distance < n_slab else []
        across = [(0, distance), (0, -distance)] if 2 * distance < n_chan else []
        rounds.append(along + across)
        distance *= 2

    def tell(index):
        for row_step, col_step in rounds[index]:
            pl.semaphore_signal(
                known.at[index],
                inc=1,
                device_id=(slab_at(row_step), chan_at(col_step)),
                device_id_type=MESH,
            )

    def hear(index):
        pl.semaphore_wait(known.at[index], len(rounds[index]))

    def send(index, source, target, row_step, col_step):
        copy = pltpu.make_async_remote_copy(
            src_ref=source,
            dst_ref=target,
            send_sem=halo_send.at[index],
            recv_sem=halo_recv.at[index],
            device_id=(slab_at(row_step), chan_at(col_step)),
            device_id_type=MESH,
        )
        copy.start()
        return copy

    slot = lax.broadcasted_iota(jnp.int32, (32, PIX), 0)
    column = lax.broadcasted_iota(jnp.int32, (32, PIX), 1)
    outer = jnp.where(column < 2, column, jnp.where(column >= PIX - 2, column + 18 - PIX, 99))

    loads[0].wait()
    loads[1].wait()

    def pack(row, carry):
        pick = jnp.where(outer + 2 * row == slot, 1.0, 0.0).astype(BF)
        return tuple(
            total + dot_nt(pick, raw[kind, row + 2]) for kind, total in enumerate(carry)
        )

    empty = jnp.zeros((32, C), F32)
    packed = lax.fori_loop(0, ROWS, pack, (empty, empty))
    for kind in range(2):
        edges[0, kind] = packed[kind][:16].astype(BF)
        edges[1, kind] = packed[kind][16:].astype(BF)

    pl.semaphore_wait(barrier, 8)
    row_copies = [
        send(0, center_in.at[pl.ds(6, 2)], raw.at[0, pl.ds(0, 2)], 1, 0),
        send(1, center_in.at[pl.ds(0, 2)], raw.at[0, pl.ds(10, 2)], -1, 0),
        send(2, radius_in.at[pl.ds(6, 2)], raw.at[1, pl.ds(0, 2)], 1, 0),
        send(3, radius_in.at[pl.ds(0, 2)], raw.at[1, pl.ds(10, 2)], -1, 0),
    ]
    side_copies = [
        send(4, edges.at[1], side.at[0, 1], 0, 1),
        send(5, edges.at[0], side.at[1, 1], 0, -1),
    ]
    corner_copies = [
        send(6, edges.at[1], side.at[0, 0], 1, 1),
        send(7, edges.at[0], side.at[1, 0], 1, -1),
        send(8, edges.at[1], side.at[0, 2], -1, 1),
        send(9, edges.at[0], side.at[1, 2], -1, -1),
    ]

    tell(0)

    place = lax.broadcasted_iota(jnp.int32, (3, PAD, PIX), 1)
    shift = lax.broadcasted_iota(jnp.int32, (3, PAD, PIX), 0)
    column = lax.broadcasted_iota(jnp.int32, (3, PAD, PIX), 2)
    select = jnp.where(place - 9 + shift == column, 1.0, 0.0).astype(BF)
    select = select.reshape(3 * PAD, PIX)

    def widen(kind, row, scale):
        turned = dot_nt(select, raw[kind, row])
        if scale is not None:
            turned = turned * scale
        turned = turned.astype(BF)
        for offset in range(3):
            wide[offset, kind, row] = turned[offset * PAD : (offset + 1) * PAD]

    def widen_own(row, carry):
        widen(0, row + 2, None)
        widen(1, row + 2, None)
        return carry

    lax.fori_loop(0, ROWS, widen_own, 0)

    above = jnp.where(s > 0, 1.0, 0.0).astype(F32)
    below = jnp.where(s < n_slab - 1, 1.0, 0.0).astype(F32)
    leftward = jnp.where(c > 0, 1.0, 0.0).astype(F32)
    rightward = jnp.where(c < n_chan - 1, 1.0, 0.0).astype(F32)

    line = lax.broadcasted_iota(jnp.int32, (16, C), 0)
    both = (line == 7) | (line == 8)

    def patch(row, group, line_at, scale):
        turn = 24 - 2 * line_at
        for kind in range(2):
            low = side[0, group, kind].astype(F32) * (scale * leftward)
            high = side[1, group, kind].astype(F32) * (scale * rightward)
            for offset, cols, mask, source, step in (
                (0, slice(0, 16), both, low, turn - 1),
                (1, slice(0, 16), line == 7, low, turn - 2),
                (1, slice(PIX, PAD), line == 8, high, turn),
                (2, slice(PIX, PAD), both, high, turn - 1),
            ):
                moved = pltpu.roll(source, step % 16, 0)
                tile = wide[offset, kind, row, cols].astype(F32)
                wide[offset, kind, row, cols] = jnp.where(mask, moved, tile).astype(BF)

    def patch_own(row, carry):
        patch(row + 2, 1, row, 1.0)
        return carry

    def layer_one(read, count, row_of):
        center = jnp.zeros((count * PAD, C), F32)
        radius = jnp.zeros((count * PAD, C), F32)
        for a in range(3):
            for b in range(3):
                weight = first[a, b]
                center = center + dot_nt(read(b, 0, a).reshape(count * PAD, C), weight)
                radius = radius + dot_nt(read(b, 1, a).reshape(count * PAD, C), jnp.abs(weight))
        middle, spread = interval_relu(center + first_bias[...], radius)
        row_at = row_of(lax.broadcasted_iota(jnp.int32, (count, PAD, C), 0)) + (s * ROWS - 1)
        col_at = lax.broadcasted_iota(jnp.int32, (count, PAD, C), 1) + (c * PIX - 8)
        inside = (
            (row_at >= 0)
            & (row_at < n_slab * ROWS)
            & (col_at >= 0)
            & (col_at < n_chan * PIX)
        )
        middle = jnp.where(inside, middle.reshape(count, PAD, C), 0.0)
        spread = jnp.where(inside, spread.reshape(count, PAD, C), 0.0)
        return middle, spread

    hear(0)
    tell(1)
    for copy in side_copies:
        copy.wait()
    lax.fori_loop(0, ROWS, patch_own, 0)
    loads[2].wait()
    hear(1)
    tell(2)

    inner = layer_one(lambda b, kind, a: wide[b, kind, 2 + a : 8 + a], 6, lambda row: row + 2)
    for kind in range(2):
        for b in range(3):
            layer[b, kind, 2:8] = inner[kind][:, 7 + b : 7 + b + PIX].astype(BF)

    hear(2)
    tell(3)
    for copy in row_copies + corner_copies:
        copy.wait()

    def widen_halo(kind, carry):
        for row in (0, 1):
            widen(kind, row, above)
        for row in (10, 11):
            widen(kind, row, below)
        return carry

    lax.fori_loop(0, 2, widen_halo, 0)

    def patch_halo(row, carry):
        patch(row, 0, row + 6, above)
        patch(row + 10, 2, row, below)
        return carry

    lax.fori_loop(0, 2, patch_halo, 0)
    outside = layer_one(
        lambda b, kind, a: jnp.concatenate(
            [wide[b, kind, a : a + 2], wide[b, kind, 8 + a : 10 + a]], axis=0
        ),
        4,
        lambda row: jnp.where(row < 2, row, row + 6),
    )
    for kind in range(2):
        for b in range(3):
            rows = outside[kind][:, 7 + b : 7 + b + PIX].astype(BF)
            layer[b, kind, 0:2] = rows[:2]
            layer[b, kind, 8:10] = rows[2:]

    hear(3)
    for load in loads[3:]:
        load.wait()

    def layer_two(read, count):
        center = jnp.zeros((count * PIX, C), F32)
        radius = jnp.zeros((count * PIX, C), F32)
        for a in range(3):
            for b in range(3):
                weight = second[a, b]
                center = center + dot_nt(read(b, 0, a), weight)
                radius = radius + dot_nt(read(b, 1, a), jnp.abs(weight))
        middle, spread = interval_relu(center + second_bias[...], radius)
        return middle.astype(BF), spread.astype(BF)

    def head(middle, spread, weight, bias):
        return dot_nt(middle, weight) + bias, dot_nt(spread, jnp.abs(weight))

    first_row = tile_row[0, 0]
    second_row = tile_row[0, 1]

    def read_tiles(b, kind, a):
        return jnp.concatenate(
            [layer[b, kind, first_row + a], layer[b, kind, second_row + a]], axis=0
        )

    middle_two, radius_two = layer_two(read_tiles, 2)
    pre_three = head(middle_two, radius_two, third[...], third_bias[...])
    slope_three, offset_three = relax_slopes(*pre_three)
    middle_three, radius_three = interval_relu(*pre_three)
    pre_four = head(
        middle_three.astype(BF), radius_three.astype(BF), fourth[...], fourth_bias[...]
    )
    slope_four, offset_four = relax_slopes(*pre_four)
    score = score_weight[...].astype(F32).reshape(1, C)
    coeff_four = (score * slope_four).astype(BF)
    carried = dot_nn(coeff_four, fourth[...])
    coeff_three = (carried * slope_three).astype(BF)
    reached = dot_nn(coeff_three, third[...])
    shared = (
        coeff_four.astype(F32) * fourth_bias[...]
        + coeff_three.astype(F32) * third_bias[...]
        + reached * middle_two.astype(F32)
    )
    reach = jnp.abs(reached) * radius_two.astype(F32)
    lower = (
        shared + jnp.minimum(score, 0.0) * offset_four + jnp.minimum(carried, 0.0) * offset_three
    ) - reach
    upper = (
        shared + jnp.maximum(score, 0.0) * offset_four + jnp.maximum(carried, 0.0) * offset_three
    ) + reach
    bias_score = score_bias[0, 0]

    def column_sum(value):
        halves = value[:, :PIX] + value[:, PIX:]
        return jnp.sum(halves.T, axis=0, keepdims=True) + bias_score

    sub = lax.broadcasted_iota(jnp.int32, (8, PIX), 0)
    blob = jnp.zeros((8, PIX), F32)
    for tile in range(2):
        rows = slice(tile * PIX, (tile + 1) * PIX)
        blob = jnp.where(sub == 2 * tile, column_sum(lower[rows]), blob)
        blob = jnp.where(sub == 2 * tile + 1, column_sum(upper[rows]), blob)
        slot = jnp.where(tile < tile_count[0, 0], owner_slot[0, tile], -1)
        blob = jnp.where(sub == 4 + tile, slot.astype(F32), blob)
    gathered[c] = blob

    def chan_copy(step):
        return pltpu.make_async_remote_copy(
            src_ref=gathered.at[c],
            dst_ref=gathered.at[c],
            send_sem=chan_send.at[step - 1],
            recv_sem=chan_recv.at[step - 1],
            device_id=(s, chan_at(step)),
            device_id_type=MESH,
        )

    for step in range(1, n_chan):
        chan_copy(step).start()

    keeper = lax.broadcasted_iota(jnp.int32, (n_slab, PIX), 0).astype(F32) * 8.0

    def collect(peer, carry):
        low, high, slots = carry
        for tile in range(2):
            slot = gathered[peer, 4 + tile : 5 + tile]
            mine = (slot >= keeper) & (slot < keeper + 8.0)
            low = jnp.where(mine, gathered[peer, 2 * tile : 2 * tile + 1], low)
            high = jnp.where(mine, gathered[peer, 2 * tile + 1 : 2 * tile + 2], high)
            slots = jnp.where(mine, slot - keeper + 1.0, slots)
        return low, high, slots

    def collect_from(step, carry):
        chan_copy(step).wait_recv()
        return collect(chan_at(n_chan - step), carry)

    empty = jnp.zeros((n_slab, PIX), F32)
    found = collect(c, (empty, empty, empty))
    low, high, slots = lax.fori_loop(1, n_chan, collect_from, found)
    message[:, 0, :] = low
    message[:, 1, :] = high
    message[:, 2, :] = slots
    arrived[s] = message[s]

    def other(index):
        return index + lax.div(index - s + n_slab, n_slab)

    def slab_copy(index):
        return pltpu.make_async_remote_copy(
            src_ref=message.at[other(index)],
            dst_ref=arrived.at[s],
            send_sem=slab_send.at[index],
            recv_sem=slab_recv.at[s],
            device_id=(other(index), c),
            device_id_type=MESH,
        )

    def slab_arrival(index):
        return pltpu.make_async_remote_copy(
            src_ref=message.at[other(index)],
            dst_ref=arrived.at[other(index)],
            send_sem=slab_send.at[index],
            recv_sem=slab_recv.at[other(index)],
            device_id=(other(index), c),
            device_id_type=MESH,
        )

    for index in range(n_slab - 1):
        slab_copy(index).start()

    n2 = 4
    score_rows = jnp.broadcast_to(score, (16, C)).astype(BF)

    def forward(part, carry):
        def read(b, kind, a):
            return layer[b, kind, pl.ds(part * n2 + a, n2)].reshape(n2 * PIX, C)

        middle, spread = layer_two(read, n2)
        middle, spread = interval_relu(*head(middle, spread, third[...], third_bias[...]))
        middle, spread = interval_relu(
            *head(middle.astype(BF), spread.astype(BF), fourth[...], fourth_bias[...])
        )
        center = dot_nt(score_rows, middle.astype(BF)) + bias_score
        radius = dot_nt(jnp.abs(score_rows), spread.astype(BF))
        low = (center - radius)[:8]
        high = (center + radius)[:8]
        for row in range(n2):
            cols = slice(row * PIX, (row + 1) * PIX)
            out[pl.ds(part * n2 + row, 1)] = low[0:1, cols]
            out[pl.ds(ROWS + part * n2 + row, 1)] = high[0:1, cols]
        return carry

    lax.fori_loop(0, 2, forward, 0)

    wanted = lax.broadcasted_iota(jnp.int32, (8, PIX), 0).astype(F32) + 1.0

    def keep(peer, carry):
        low, high = carry
        mine = arrived[peer, 2:3] == wanted
        return (
            jnp.where(mine, arrived[peer, 0:1], low),
            jnp.where(mine, arrived[peer, 1:2], high),
        )

    empty = jnp.zeros((8, PIX), F32)

    def keep_from(index, carry):
        slab_arrival(index).wait_recv()
        return keep(other(index), carry)

    low, high = lax.fori_loop(0, n_slab - 1, keep_from, keep(s, (empty, empty)))
    out[16:24] = low
    out[24:32] = high

    def chan_sent(step, carry):
        chan_copy(step).wait_send()
        return carry

    def slab_sent(index, carry):
        slab_copy(index).wait_send()
        return carry

    lax.fori_loop(1, n_chan, chan_sent, 0)
    lax.fori_loop(0, n_slab - 1, slab_sent, 0)


def unpack(bounds, ibp_out, refined_out):
    ibp_out[0] = bounds[0:8]
    ibp_out[1] = bounds[8:16]
    refined_out[:, 0, :] = bounds[16:24]
    refined_out[:, 1, :] = bounds[24:32]


def solution(mesh):
    n_slab = mesh.shape["slab"]
    n_chan = mesh.shape["chan"]

    def body(
        image_center,
        image_radius,
        first_kernel,
        first_bias,
        second_kernel,
        second_bias,
        third_weight,
        third_bias,
        fourth_weight,
        fourth_bias,
        score_weight,
        score_bias,
        tile_count,
        tile_row,
        owner_slot,
    ):
        hbm = pl.BlockSpec(memory_space=pl.ANY)
        vmem = pl.BlockSpec(memory_space=pltpu.VMEM)
        smem = pl.BlockSpec(memory_space=pltpu.SMEM)
        dma = pltpu.SemaphoreType.DMA
        bounds = pl.pallas_call(
            functools.partial(kernel, n_slab, n_chan),
            out_shape=jax.ShapeDtypeStruct((32, PIX), F32),
            in_specs=[hbm] * 6 + [vmem] * 5 + [smem] * 4,
            out_specs=vmem,
            scratch_shapes=[
                pltpu.VMEM((2, ROWS + 4, C, PIX), BF),
                pltpu.VMEM((3, 2, ROWS + 4, PAD, C), BF),
                pltpu.VMEM((2, 2, 16, C), BF),
                pltpu.VMEM((2, 3, 2, 16, C), BF),
                pltpu.VMEM((3, 2, ROWS + 2, PIX, C), BF),
                pltpu.VMEM((3, 3, C, C), BF),
                pltpu.VMEM((3, 3, C, C), BF),
                pltpu.VMEM((C, C), BF),
                pltpu.VMEM((C, C), BF),
                pltpu.VMEM((n_chan, 8, PIX), F32),
                pltpu.VMEM((n_slab, 3, PIX), F32),
                pltpu.VMEM((n_slab, 3, PIX), F32),
                pltpu.SemaphoreType.REGULAR((4,)),
                dma((6,)),
                dma((10,)),
                dma((10,)),
                dma((n_chan - 1,)),
                dma((n_chan - 1,)),
                dma((n_slab - 1,)),
                dma((n_slab,)),
            ],
            compiler_params=pltpu.CompilerParams(
                collective_id=0, has_side_effects=True, vmem_limit_bytes=56 * 1024 * 1024
            ),
        )(
            image_center,
            image_radius,
            first_kernel,
            second_kernel,
            third_weight,
            fourth_weight,
            first_bias[None, :],
            second_bias[None, :],
            third_bias[None, :],
            fourth_bias[None, :],
            score_weight,
            score_bias[None, :],
            tile_count,
            tile_row[0],
            owner_slot[0],
        )
        return pl.pallas_call(
            unpack,
            out_shape=(
                jax.ShapeDtypeStruct((2, ROWS, PIX), F32),
                jax.ShapeDtypeStruct((8, 2, PIX), F32),
            ),
            in_specs=[vmem],
            out_specs=(vmem, vmem),
        )(bounds)

    placed = (
        P("slab", None, "chan"),
        P("slab", None, "chan"),
        *(P(),) * 10,
        P("slab", "chan"),
        P("slab", "chan", None),
        P("slab", "chan", None),
    )
    return jax.shard_map(
        body,
        mesh=mesh,
        in_specs=placed,
        out_specs=(P(None, "slab", "chan"), P("slab", None, None)),
        check_vma=False,
    )
```

```python
import functools

import jax
import jax.numpy as jnp
from jax import lax
from jax.experimental import pallas as pl
from jax.experimental.pallas import tpu as pltpu
from jax.sharding import PartitionSpec as P

EPSILON = 1e-06
MESH = pl.DeviceIdType.MESH
BF = jnp.bfloat16
F32 = jnp.float32
C = 256
PIX = 128
ROWS = 8
PAD = 144


def dot_nt(lhs, rhs):
    return lax.dot_general(lhs, rhs, (((1,), (1,)), ((), ())), preferred_element_type=F32)


def dot_nn(lhs, rhs):
    return lax.dot_general(lhs, rhs, (((1,), (0,)), ((), ())), preferred_element_type=F32)


def interval_relu(center, radius):
    lower = jnp.maximum(center - radius, 0.0)
    upper = jnp.maximum(center + radius, 0.0)
    return (lower + upper) * 0.5, (upper - lower) * 0.5


def relax_slopes(center, radius):
    upper = jnp.maximum(center + radius, 0.0)
    below = jnp.maximum(radius - center, 0.0)
    slope = upper / (upper + below + EPSILON)
    return slope.astype(BF).astype(F32), (slope * below).astype(BF).astype(F32)


def kernel(
    n_slab,
    n_chan,
    center_in,
    radius_in,
    first_in,
    second_in,
    third_in,
    fourth_in,
    first_bias,
    second_bias,
    third_bias,
    fourth_bias,
    score_weight,
    score_bias,
    tile_count,
    tile_row,
    owner_slot,
    out,
    raw,
    wide,
    edges,
    side,
    layer,
    first,
    second,
    third,
    fourth,
    gathered,
    message,
    arrived,
    known,
    local_sem,
    halo_send,
    halo_recv,
    chan_send,
    chan_recv,
    slab_send,
    slab_recv,
):
    s = lax.axis_index("slab")
    c = lax.axis_index("chan")

    def slab_at(step):
        return lax.rem(s + step + n_slab, n_slab)

    def chan_at(step):
        return lax.rem(c + step + n_chan, n_chan)

    loads = [
        pltpu.make_async_copy(center_in, raw.at[0, pl.ds(2, ROWS)], local_sem.at[0]),
        pltpu.make_async_copy(radius_in, raw.at[1, pl.ds(2, ROWS)], local_sem.at[1]),
        pltpu.make_async_copy(first_in, first, local_sem.at[2]),
        pltpu.make_async_copy(second_in, second, local_sem.at[3]),
        pltpu.make_async_copy(third_in, third, local_sem.at[4]),
        pltpu.make_async_copy(fourth_in, fourth, local_sem.at[5]),
    ]
    for load in loads:
        load.start()

    barrier = pltpu.get_barrier_semaphore()

    def greet(row_step, col_step):
        pl.semaphore_signal(
            barrier,
            inc=1,
            device_id=(slab_at(row_step), chan_at(col_step)),
            device_id_type=MESH,
        )

    for row_step in (-1, 0, 1):
        for col_step in (-1, 0, 1):
            if row_step or col_step:
                greet(row_step, col_step)

    rounds = []
    distance = 1
    while 2 * distance < max(n_slab, n_chan):
        along = [(distance, 0), (-distance, 0)] if 2 * distance < n_slab else []
        across = [(0, distance), (0, -distance)] if 2 * distance < n_chan else []
        rounds.append(along + across)
        distance *= 2

    def tell(index):
        for row_step, col_step in rounds[index]:
            pl.semaphore_signal(
                known.at[index],
                inc=1,
                device_id=(slab_at(row_step), chan_at(col_step)),
                device_id_type=MESH,
            )

    def hear(index):
        pl.semaphore_wait(known.at[index], len(rounds[index]))

    def send(index, source, target, row_step, col_step):
        copy = pltpu.make_async_remote_copy(
            src_ref=source,
            dst_ref=target,
            send_sem=halo_send.at[index],
            recv_sem=halo_recv.at[index],
            device_id=(slab_at(row_step), chan_at(col_step)),
            device_id_type=MESH,
        )
        copy.start()
        return copy

    slot = lax.broadcasted_iota(jnp.int32, (32, PIX), 0)
    column = lax.broadcasted_iota(jnp.int32, (32, PIX), 1)
    outer = jnp.where(column < 2, column, jnp.where(column >= PIX - 2, column + 18 - PIX, 99))

    loads[0].wait()
    loads[1].wait()

    def pack(row, carry):
        pick = jnp.where(outer + 2 * row == slot, 1.0, 0.0).astype(BF)
        return tuple(
            total + dot_nt(pick, raw[kind, row + 2]) for kind, total in enumerate(carry)
        )

    empty = jnp.zeros((32, C), F32)
    packed = lax.fori_loop(0, ROWS, pack, (empty, empty))
    for kind in range(2):
        edges[0, kind] = packed[kind][:16].astype(BF)
        edges[1, kind] = packed[kind][16:].astype(BF)

    pl.semaphore_wait(barrier, 8)
    row_copies = [
        send(0, center_in.at[pl.ds(6, 2)], raw.at[0, pl.ds(0, 2)], 1, 0),
        send(1, center_in.at[pl.ds(0, 2)], raw.at[0, pl.ds(10, 2)], -1, 0),
        send(2, radius_in.at[pl.ds(6, 2)], raw.at[1, pl.ds(0, 2)], 1, 0),
        send(3, radius_in.at[pl.ds(0, 2)], raw.at[1, pl.ds(10, 2)], -1, 0),
    ]
    side_copies = [
        send(4, edges.at[1], side.at[0, 1], 0, 1),
        send(5, edges.at[0], side.at[1, 1], 0, -1),
    ]
    corner_copies = [
        send(6, edges.at[1], side.at[0, 0], 1, 1),
        send(7, edges.at[0], side.at[1, 0], 1, -1),
        send(8, edges.at[1], side.at[0, 2], -1, 1),
        send(9, edges.at[0], side.at[1, 2], -1, -1),
    ]

    tell(0)

    place = lax.broadcasted_iota(jnp.int32, (3, PAD, PIX), 1)
    shift = lax.broadcasted_iota(jnp.int32, (3, PAD, PIX), 0)
    column = lax.broadcasted_iota(jnp.int32, (3, PAD, PIX), 2)
    select = jnp.where(place - 9 + shift == column, 1.0, 0.0).astype(BF)
    select = select.reshape(3 * PAD, PIX)

    def widen(kind, row, scale):
        turned = dot_nt(select, raw[kind, row])
        if scale is not None:
            turned = turned * scale
        turned = turned.astype(BF)
        for offset in range(3):
            wide[offset, kind, row] = turned[offset * PAD : (offset + 1) * PAD]

    def widen_own(row, carry):
        widen(0, row + 2, None)
        widen(1, row + 2, None)
        return carry

    lax.fori_loop(0, ROWS, widen_own, 0)

    above = jnp.where(s > 0, 1.0, 0.0).astype(F32)
    below = jnp.where(s < n_slab - 1, 1.0, 0.0).astype(F32)
    leftward = jnp.where(c > 0, 1.0, 0.0).astype(F32)
    rightward = jnp.where(c < n_chan - 1, 1.0, 0.0).astype(F32)

    line = lax.broadcasted_iota(jnp.int32, (16, C), 0)
    both = (line == 7) | (line == 8)

    def patch(row, group, line_at, scale):
        turn = 24 - 2 * line_at
        for kind in range(2):
            low = side[0, group, kind].astype(F32) * (scale * leftward)
            high = side[1, group, kind].astype(F32) * (scale * rightward)
            for offset, cols, mask, source, step in (
                (0, slice(0, 16), both, low, turn - 1),
                (1, slice(0, 16), line == 7, low, turn - 2),
                (1, slice(PIX, PAD), line == 8, high, turn),
                (2, slice(PIX, PAD), both, high, turn - 1),
            ):
                moved = pltpu.roll(source, step % 16, 0)
                tile = wide[offset, kind, row, cols].astype(F32)
                wide[offset, kind, row, cols] = jnp.where(mask, moved, tile).astype(BF)

    def patch_own(row, carry):
        patch(row + 2, 1, row, 1.0)
        return carry

    def layer_one(read, count, row_of):
        center = jnp.zeros((count * PAD, C), F32)
        radius = jnp.zeros((count * PAD, C), F32)
        for a in range(3):
            for b in range(3):
                weight = first[a, b]
                center = center + dot_nt(read(b, 0, a).reshape(count * PAD, C), weight)
                radius = radius + dot_nt(read(b, 1, a).reshape(count * PAD, C), jnp.abs(weight))
        middle, spread = interval_relu(center + first_bias[...], radius)
        row_at = row_of(lax.broadcasted_iota(jnp.int32, (count, PAD, C), 0)) + (s * ROWS - 1)
        col_at = lax.broadcasted_iota(jnp.int32, (count, PAD, C), 1) + (c * PIX - 8)
        inside = (
            (row_at >= 0)
            & (row_at < n_slab * ROWS)
            & (col_at >= 0)
            & (col_at < n_chan * PIX)
        )
        middle = jnp.where(inside, middle.reshape(count, PAD, C), 0.0)
        spread = jnp.where(inside, spread.reshape(count, PAD, C), 0.0)
        return middle, spread

    hear(0)
    tell(1)
    for copy in side_copies:
        copy.wait()
    lax.fori_loop(0, ROWS, patch_own, 0)
    loads[2].wait()
    hear(1)
    tell(2)

    inner = layer_one(lambda b, kind, a: wide[b, kind, 2 + a : 8 + a], 6, lambda row: row + 2)
    for kind in range(2):
        for b in range(3):
            layer[b, kind, 2:8] = inner[kind][:, 7 + b : 7 + b + PIX].astype(BF)

    hear(2)
    tell(3)
    for copy in row_copies + corner_copies:
        copy.wait()

    def widen_halo(kind, carry):
        for row in (0, 1):
            widen(kind, row, above)
        for row in (10, 11):
            widen(kind, row, below)
        return carry

    lax.fori_loop(0, 2, widen_halo, 0)

    def patch_halo(row, carry):
        patch(row, 0, row + 6, above)
        patch(row + 10, 2, row, below)
        return carry

    lax.fori_loop(0, 2, patch_halo, 0)
    outside = layer_one(
        lambda b, kind, a: jnp.concatenate(
            [wide[b, kind, a : a + 2], wide[b, kind, 8 + a : 10 + a]], axis=0
        ),
        4,
        lambda row: jnp.where(row < 2, row, row + 6),
    )
    for kind in range(2):
        for b in range(3):
            rows = outside[kind][:, 7 + b : 7 + b + PIX].astype(BF)
            layer[b, kind, 0:2] = rows[:2]
            layer[b, kind, 8:10] = rows[2:]

    hear(3)
    for load in loads[3:]:
        load.wait()

    def layer_two(read, count):
        center = jnp.zeros((count * PIX, C), F32)
        radius = jnp.zeros((count * PIX, C), F32)
        for a in range(3):
            for b in range(3):
                weight = second[a, b]
                center = center + dot_nt(read(b, 0, a), weight)
                radius = radius + dot_nt(read(b, 1, a), jnp.abs(weight))
        middle, spread = interval_relu(center + second_bias[...], radius)
        return middle.astype(BF), spread.astype(BF)

    def head(middle, spread, weight, bias):
        return dot_nt(middle, weight) + bias, dot_nt(spread, jnp.abs(weight))

    first_row = tile_row[0, 0]
    second_row = tile_row[0, 1]

    def read_tiles(b, kind, a):
        return jnp.concatenate(
            [layer[b, kind, first_row + a], layer[b, kind, second_row + a]], axis=0
        )

    middle_two, radius_two = layer_two(read_tiles, 2)
    pre_three = head(middle_two, radius_two, third[...], third_bias[...])
    slope_three, offset_three = relax_slopes(*pre_three)
    middle_three, radius_three = interval_relu(*pre_three)
    pre_four = head(
        middle_three.astype(BF), radius_three.astype(BF), fourth[...], fourth_bias[...]
    )
    slope_four, offset_four = relax_slopes(*pre_four)
    score = score_weight[...].astype(F32).reshape(1, C)
    coeff_four = (score * slope_four).astype(BF)
    carried = dot_nn(coeff_four, fourth[...])
    coeff_three = (carried * slope_three).astype(BF)
    reached = dot_nn(coeff_three, third[...])
    shared = (
        coeff_four.astype(F32) * fourth_bias[...]
        + coeff_three.astype(F32) * third_bias[...]
        + reached * middle_two.astype(F32)
    )
    reach = jnp.abs(reached) * radius_two.astype(F32)
    lower = (
        shared + jnp.minimum(score, 0.0) * offset_four + jnp.minimum(carried, 0.0) * offset_three
    ) - reach
    upper = (
        shared + jnp.maximum(score, 0.0) * offset_four + jnp.maximum(carried, 0.0) * offset_three
    ) + reach
    bias_score = score_bias[0, 0]

    def column_sum(value):
        halves = value[:, :PIX] + value[:, PIX:]
        return jnp.sum(halves.T, axis=0, keepdims=True) + bias_score

    sub = lax.broadcasted_iota(jnp.int32, (8, PIX), 0)
    blob = jnp.zeros((8, PIX), F32)
    for tile in range(2):
        rows = slice(tile * PIX, (tile + 1) * PIX)
        blob = jnp.where(sub == 2 * tile, column_sum(lower[rows]), blob)
        blob = jnp.where(sub == 2 * tile + 1, column_sum(upper[rows]), blob)
        slot = jnp.where(tile < tile_count[0, 0], owner_slot[0, tile], -1)
        blob = jnp.where(sub == 4 + tile, slot.astype(F32), blob)
    gathered[c] = blob

    def chan_copy(step):
        return pltpu.make_async_remote_copy(
            src_ref=gathered.at[c],
            dst_ref=gathered.at[c],
            send_sem=chan_send.at[step - 1],
            recv_sem=chan_recv.at[step - 1],
            device_id=(s, chan_at(step)),
            device_id_type=MESH,
        )

    for step in range(1, n_chan):
        chan_copy(step).start()

    keeper = lax.broadcasted_iota(jnp.int32, (n_slab, PIX), 0).astype(F32) * 8.0

    def collect(peer, carry):
        low, high, slots = carry
        for tile in range(2):
            slot = gathered[peer, 4 + tile : 5 + tile]
            mine = (slot >= keeper) & (slot < keeper + 8.0)
            low = jnp.where(mine, gathered[peer, 2 * tile : 2 * tile + 1], low)
            high = jnp.where(mine, gathered[peer, 2 * tile + 1 : 2 * tile + 2], high)
            slots = jnp.where(mine, slot - keeper + 1.0, slots)
        return low, high, slots

    def collect_from(step, carry):
        chan_copy(step).wait_recv()
        return collect(chan_at(n_chan - step), carry)

    empty = jnp.zeros((n_slab, PIX), F32)
    found = collect(c, (empty, empty, empty))
    low, high, slots = lax.fori_loop(1, n_chan, collect_from, found)
    message[:, 0, :] = low
    message[:, 1, :] = high
    message[:, 2, :] = slots
    arrived[s] = message[s]

    def other(index):
        return index + lax.div(index - s + n_slab, n_slab)

    def slab_copy(index):
        return pltpu.make_async_remote_copy(
            src_ref=message.at[other(index)],
            dst_ref=arrived.at[s],
            send_sem=slab_send.at[index],
            recv_sem=slab_recv.at[s],
            device_id=(other(index), c),
            device_id_type=MESH,
        )

    def slab_arrival(index):
        return pltpu.make_async_remote_copy(
            src_ref=message.at[other(index)],
            dst_ref=arrived.at[other(index)],
            send_sem=slab_send.at[index],
            recv_sem=slab_recv.at[other(index)],
            device_id=(other(index), c),
            device_id_type=MESH,
        )

    for index in range(n_slab - 1):
        slab_copy(index).start()

    n2 = 4
    score_rows = jnp.broadcast_to(score, (16, C)).astype(BF)

    def forward(part, carry):
        def read(b, kind, a):
            return layer[b, kind, pl.ds(part * n2 + a, n2)].reshape(n2 * PIX, C)

        middle, spread = layer_two(read, n2)
        middle, spread = interval_relu(*head(middle, spread, third[...], third_bias[...]))
        middle, spread = interval_relu(
            *head(middle.astype(BF), spread.astype(BF), fourth[...], fourth_bias[...])
        )
        center = dot_nt(score_rows, middle.astype(BF)) + bias_score
        radius = dot_nt(jnp.abs(score_rows), spread.astype(BF))
        low = (center - radius)[:8]
        high = (center + radius)[:8]
        for row in range(n2):
            cols = slice(row * PIX, (row + 1) * PIX)
            out[pl.ds(part * n2 + row, 1)] = low[0:1, cols]
            out[pl.ds(ROWS + part * n2 + row, 1)] = high[0:1, cols]
        return carry

    lax.fori_loop(0, 2, forward, 0)

    def chan_sent(step, carry):
        chan_copy(step).wait_send()
        return carry

    def slab_sent(index, carry):
        slab_copy(index).wait_send()
        return carry

    lax.fori_loop(1, n_chan, chan_sent, 0)
    lax.fori_loop(0, n_slab - 1, slab_sent, 0)

    wanted = lax.broadcasted_iota(jnp.int32, (8, PIX), 0).astype(F32) + 1.0

    def keep(peer, carry):
        low, high = carry
        mine = arrived[peer, 2:3] == wanted
        return (
            jnp.where(mine, arrived[peer, 0:1], low),
            jnp.where(mine, arrived[peer, 1:2], high),
        )

    empty = jnp.zeros((8, PIX), F32)

    def keep_from(index, carry):
        slab_arrival(index).wait_recv()
        return keep(other(index), carry)

    low, high = lax.fori_loop(0, n_slab - 1, keep_from, keep(s, (empty, empty)))
    out[16:24] = low
    out[24:32] = high


def unpack(bounds, ibp_out, refined_out):
    ibp_out[0] = bounds[0:8]
    ibp_out[1] = bounds[8:16]
    refined_out[:, 0, :] = bounds[16:24]
    refined_out[:, 1, :] = bounds[24:32]


def solution(mesh):
    n_slab = mesh.shape["slab"]
    n_chan = mesh.shape["chan"]

    def body(
        image_center,
        image_radius,
        first_kernel,
        first_bias,
        second_kernel,
        second_bias,
        third_weight,
        third_bias,
        fourth_weight,
        fourth_bias,
        score_weight,
        score_bias,
        tile_count,
        tile_row,
        owner_slot,
    ):
        hbm = pl.BlockSpec(memory_space=pl.ANY)
        vmem = pl.BlockSpec(memory_space=pltpu.VMEM)
        smem = pl.BlockSpec(memory_space=pltpu.SMEM)
        dma = pltpu.SemaphoreType.DMA
        bounds = pl.pallas_call(
            functools.partial(kernel, n_slab, n_chan),
            out_shape=jax.ShapeDtypeStruct((32, PIX), F32),
            in_specs=[hbm] * 6 + [vmem] * 5 + [smem] * 4,
            out_specs=vmem,
            scratch_shapes=[
                pltpu.VMEM((2, ROWS + 4, C, PIX), BF),
                pltpu.VMEM((3, 2, ROWS + 4, PAD, C), BF),
                pltpu.VMEM((2, 2, 16, C), BF),
                pltpu.VMEM((2, 3, 2, 16, C), BF),
                pltpu.VMEM((3, 2, ROWS + 2, PIX, C), BF),
                pltpu.VMEM((3, 3, C, C), BF),
                pltpu.VMEM((3, 3, C, C), BF),
                pltpu.VMEM((C, C), BF),
                pltpu.VMEM((C, C), BF),
                pltpu.VMEM((n_chan, 8, PIX), F32),
                pltpu.VMEM((n_slab, 3, PIX), F32),
                pltpu.VMEM((n_slab, 3, PIX), F32),
                pltpu.SemaphoreType.REGULAR((4,)),
                dma((6,)),
                dma((10,)),
                dma((10,)),
                dma((n_chan - 1,)),
                dma((n_chan - 1,)),
                dma((n_slab - 1,)),
                dma((n_slab,)),
            ],
            compiler_params=pltpu.CompilerParams(
                collective_id=0, has_side_effects=True, vmem_limit_bytes=56 * 1024 * 1024
            ),
        )(
            image_center,
            image_radius,
            first_kernel,
            second_kernel,
            third_weight,
            fourth_weight,
            first_bias[None, :],
            second_bias[None, :],
            third_bias[None, :],
            fourth_bias[None, :],
            score_weight,
            score_bias[None, :],
            tile_count,
            tile_row[0],
            owner_slot[0],
        )
        return pl.pallas_call(
            unpack,
            out_shape=(
                jax.ShapeDtypeStruct((2, ROWS, PIX), F32),
                jax.ShapeDtypeStruct((8, 2, PIX), F32),
            ),
            in_specs=[vmem],
            out_specs=(vmem, vmem),
        )(bounds)

    placed = (
        P("slab", None, "chan"),
        P("slab", None, "chan"),
        *(P(),) * 10,
        P("slab", "chan"),
        P("slab", "chan", None),
        P("slab", "chan", None),
    )
    return jax.shard_map(
        body,
        mesh=mesh,
        in_specs=placed,
        out_specs=(P(None, "slab", "chan"), P("slab", None, None)),
        check_vma=False,
    )
```
